128 devices in a mesh: col: 16 (over y_lo, z, core), row: 8 (over y_hi, x).
Axes of the slice: x: 4, y: 4 (y_hi: 2, y_lo: 2; y = y_hi * 2 + y_lo), z: 4, core: 2. Of those that a mesh axis runs over, the one named last changes fastest.
Arguments:
- matrix: float32 [8192, 8192], P('row', 'col'), may hold values from -64 to 64, as said below
- plan: int32 [3, 16], replicated, may hold values from 0 to 1
Outputs:
- rotated: float32 [8192, 8192], P('row', 'col')
- coupling: float32 [3], replicated
The draws below stay inside these ranges and needn't reach their ends.
Inputs may be any that keep to these rules, and one draw needn't show every extreme that they name: Entries of the matrix are real numbers; column scales differ between columns.
All inputs are finite; a program needn't handle non-finite values.
Results may differ from the reference program's by a relative error of at most 0.0003.
Values sent between devices are 32-bit elements; how exact they have to be, the bound alone decides.
No kernel may reach another device: no remote copies, remote signals or barrier semaphores. Data moves between devices by JAX's collectives and lax.ppermute only.
A program may use at most 128 MiB of HBM per device.

```python
import jax
import jax.numpy as jnp
from jax import lax

BLOCK = 256
SWEEPS = 2
STEPS = 3
ROWS = 8192
COLS = 8192
N_COL = 16


def draw_matrix(key, part):
    key_base = jax.random.fold_in(key, 11)
    key_cols = jax.random.fold_in(key, 12)
    column = jnp.arange(COLS).astype(jnp.float32)
    rising = 1.0 + 3.0 * column / COLS
    rough = jnp.exp(jax.random.uniform(key_cols, (COLS,), jnp.float32, -0.7, 0.7))
    base = jnp.clip(jax.random.normal(key_base, (ROWS, COLS), jnp.float32), -6.0, 6.0)
    values = base * (rough * rising)[None, :]
    return jnp.clip(values, -64.0, 64.0)


def set_ends(array, key, least, largest):
    index_at = [jax.random.randint(jax.random.fold_in(key, axis), (), 0, length) for axis, length in enumerate(array.shape)]
    longest = array.shape.index(max(array.shape))
    neighbour = index_at[:longest] + [(index_at[longest] + 1) % array.shape[longest]] + index_at[longest + 1:]
    return array.at[tuple(index_at)].set(least).at[tuple(neighbour)].set(largest)


def setup_inputs(seed: int = 0) -> dict:
    key_list = jax.random.split(jax.random.key(seed), 3)
    return {
        "matrix": draw_matrix(jax.random.fold_in(key_list[2], 71), 0),
        "plan": set_ends(jax.random.randint(key_list[1], (STEPS, N_COL), 0, 2), jax.random.fold_in(key_list[1], 1), 0, 1).astype(jnp.int32),
    }


highest = lax.Precision.HIGHEST
eps = 1e-06

def product(first, second):
    return jnp.dot(first, second, precision=highest, preferred_element_type=jnp.float32)

def sweep_rotation(gram):
    width = gram.shape[0]
    eye = jnp.eye(width, dtype=jnp.float32)
    upper = jnp.triu(jnp.ones((width, width), jnp.float32), 1)
    rotation = eye
    for sweep in range(SWEEPS):
        diag = jnp.diagonal(gram)
        ratio = gram / (diag[:, None] + diag[None, :] + eps) * upper
        skew_raw = ratio - ratio.T
        scale = jnp.maximum(jnp.sqrt(jnp.sum(skew_raw * skew_raw)), 1.0)
        skew = skew_raw / scale
        square = product(skew, skew)
        system = eye - square
        inverse = 4.0 / 3.0 * eye - 4.0 / 9.0 * system
        for turn in range(2):
            inverse = product(inverse, 2.0 * eye - product(system, inverse))
        qmat = product(eye - 2.0 * skew + square, inverse)
        gram = product(qmat.T, product(gram, qmat))
        if sweep == 0:
            rotation = qmat
        else:
            rotation = product(rotation, qmat)
    return (rotation, gram)

def rotate_pair(pair):
    gram = lax.dot_general(pair, pair, (((0,), (0,)), ((), ())), precision=highest, preferred_element_type=jnp.float32)
    rotation, turned = sweep_rotation(gram)
    moved = product(pair, rotation)
    cross_sq = jnp.sum(turned[:BLOCK, BLOCK:] * turned[:BLOCK, BLOCK:])
    diag_sq = jnp.sum(jnp.diagonal(turned) ** 2)
    return (moved, cross_sq, diag_sq)

def reference(matrix, plan):
    pairs = matrix.reshape(ROWS, N_COL, 2 * BLOCK).transpose(1, 0, 2)
    values = []
    for step in range(STEPS):
        moved, cross_sq, diag_sq = lax.map(rotate_pair, pairs)
        values.append(jnp.log(jnp.sum(cross_sq) / jnp.sum(diag_sq)))
        left = moved[:, :, :BLOCK]
        right = moved[:, :, BLOCK:]
        flag = (plan[step] == 1)[:, None, None]
        send = jnp.where(flag, right, left)
        keep = jnp.where(flag, left, right)
        received = jnp.roll(send, 1, axis=0)
        pairs = jnp.concatenate([keep, received], axis=2)
    rotated = pairs.transpose(1, 0, 2).reshape(ROWS, COLS)
    return (rotated, jnp.stack(values).astype(jnp.float32))
```

```python
import functools

import jax
import jax.numpy as jnp
from jax import lax
from jax.experimental import pallas as pl
from jax.experimental.pallas import tpu as pltpu
from jax.sharding import PartitionSpec as P

SWEEPS = 2
STEPS = 3
TILE = 128
VMEM_LIMIT = 56 * 2**20

f32 = jnp.float32
bf16 = jnp.bfloat16
eps = 1e-06
in_vmem = pl.BlockSpec(memory_space=pltpu.VMEM)
in_smem = pl.BlockSpec(memory_space=pltpu.SMEM)


def split(x):
    high = x.astype(bf16)
    return high, (x - high.astype(f32)).astype(bf16)


def dot(first, second):
    return jnp.dot(first, second, preferred_element_type=f32)


def dot_t(first, second):
    return lax.dot_general(first, second, (((0,), (0,)), ((), ())), preferred_element_type=f32)


def triple(op, first, second):
    return op(first[0], second[0]) + (op(first[0], second[1]) + op(first[1], second[0]))


mul = functools.partial(triple, dot)
mul_t = functools.partial(triple, dot_t)


def columns(parts, start, size):
    return tuple(part[:, start : start + size] for part in parts)


def call(body, outs, in_specs, flops, name, **kwargs):
    return pl.pallas_call(
        body,
        out_shape=outs,
        in_specs=in_specs,
        out_specs=jax.tree.map(lambda _: in_vmem, outs),
        compiler_params=pltpu.CompilerParams(vmem_limit_bytes=VMEM_LIMIT),
        cost_estimate=pl.CostEstimate(flops=flops, bytes_accessed=4 * 2**20, transcendentals=0),
        name=name,
        **kwargs,
    )


def shape(*dims):
    return jax.ShapeDtypeStruct(dims, f32)


def tile_pairs(width):
    count = width // TILE
    return [(i, j) for i in range(count) for j in range(i, count)]


def gram_body(pair_ref, out_ref):
    parts = split(pair_ref[...])
    width = pair_ref.shape[1]
    half = width // 2
    blocks = {}
    for i, j in ((0, 0), (0, 1), (1, 1)):
        blocks[i, j] = mul_t(columns(parts, i * half, half), columns(parts, j * half, half))
    per = half // TILE
    for at, (i, j) in enumerate(tile_pairs(width)):
        block = blocks[i // per, j // per]
        r, c = (i % per) * TILE, (j % per) * TILE
        out_ref[at * TILE : (at + 1) * TILE, :] = block[r : r + TILE, c : c + TILE]


def local_gram(pair):
    rows, width = pair.shape
    count = len(tile_pairs(width))
    return call(gram_body, shape(count * TILE, TILE), [in_vmem], 6 * rows * width * width, "local_gram")(pair)


def cross_body(first_ref, second_ref, out_ref):
    out_ref[...] = mul_t(split(first_ref[...]), split(second_ref[...]))


def local_cross(first, second):
    rows, block = first.shape
    return call(cross_body, shape(block, block), [in_vmem] * 2, 6 * rows * block * block, "local_cross")(first, second)


def sweep(gram, row, col):
    eye = row == col
    one = eye.astype(f32)
    on_diag = jnp.where(eye, gram, 0.0)
    diag_sum = jnp.sum(on_diag, axis=0, keepdims=True) + jnp.sum(on_diag, axis=1, keepdims=True)
    ratio = gram / (diag_sum + eps)
    skew = jnp.where(col > row, ratio, jnp.where(row > col, -ratio, 0.0))
    norm = jnp.sum(jnp.sum(skew * skew, axis=0, keepdims=True), axis=1, keepdims=True)
    skew = skew * (1.0 / jnp.maximum(jnp.sqrt(norm), 1.0))
    skew_parts = split(skew)
    square = mul(skew_parts, skew_parts)
    t1 = one * (1.0 / 3.0) + square * (2.0 / 3.0)
    t1_parts = split(t1)
    t2 = mul(t1_parts, t1_parts)
    t2_parts = split(t2)
    t4 = mul(t2_parts, t2_parts)
    low = one + t1 + t2 + mul(t1_parts, t2_parts)
    inverse = (low + mul(split(low), split(t4))) * (2.0 / 3.0)
    qmat = mul(split(one - 2.0 * skew + square), split(inverse))
    q_parts = split(qmat)
    return qmat, q_parts, mul(split(gram), q_parts)


def rotate(gram, pair_left, pair_right, flag, outs):
    send_ref, keep_rot_ref, send_diag_ref, keep_diag_ref, stat_ref = outs
    width = gram.shape[0]
    half = width // 2
    row = lax.broadcasted_iota(jnp.int32, (width, width), 0)
    col = lax.broadcasted_iota(jnp.int32, (width, width), 1)
    _, first, half_turned = sweep(gram, row, col)
    gram = mul_t(first, split(half_turned))
    _, second, half_turned = sweep(gram, row, col)
    rotation = mul(first, second)
    turned = split(half_turned)
    left, right = columns(second, 0, half), columns(second, half, half)
    left_diag = mul_t(left, columns(turned, 0, half))
    right_diag = mul_t(right, columns(turned, half, half))
    cross = mul_t(left, columns(turned, half, half))
    cross_sq = jnp.sum(jnp.sum(cross * cross, axis=0, keepdims=True), axis=1, keepdims=True)
    eye = row[:half, :half] == col[:half, :half]
    on_diag = jnp.where(eye, left_diag * left_diag + right_diag * right_diag, 0.0)
    diag_sq = jnp.sum(jnp.sum(on_diag, axis=0, keepdims=True), axis=1, keepdims=True)
    lane = lax.broadcasted_iota(jnp.int32, stat_ref.shape, 1)
    stat_ref[...] = jnp.where(lane == 0, cross_sq, jnp.where(lane == 1, diag_sq, 0.0))
    send_rot = jnp.where(flag, rotation[:, half:], rotation[:, :half])
    keep_rot_ref[...] = jnp.where(flag, rotation[:, :half], rotation[:, half:])
    send_diag_ref[...] = jnp.where(flag, right_diag, left_diag)
    keep_diag_ref[...] = jnp.where(flag, left_diag, right_diag)
    rot = split(send_rot)
    top, bottom = tuple(p[:half] for p in rot), tuple(p[half:] for p in rot)
    send_ref[...] = mul(split(pair_left), top) + mul(split(pair_right), bottom)


def first_body(flag_ref, tiles_ref, pair_ref, *refs):
    outs, gram_ref = refs[:-1], refs[-1]
    width = pair_ref.shape[1]
    half = width // 2
    for at, (i, j) in enumerate(tile_pairs(width)):
        tile = tiles_ref[at * TILE : (at + 1) * TILE, :]
        gram_ref[i * TILE : (i + 1) * TILE, j * TILE : (j + 1) * TILE] = tile
        if i != j:
            gram_ref[j * TILE : (j + 1) * TILE, i * TILE : (i + 1) * TILE] = tile.T
    flag = flag_ref[0] == 1
    rotate(gram_ref[...], pair_ref[:, :half], pair_ref[:, half:], flag, outs)


def later_body(flag_ref, left_diag_ref, cross_ref, right_diag_ref, left_ref, right_ref, *refs):
    outs, gram_ref = refs[:-1], refs[-1]
    half = cross_ref.shape[0]
    cross = cross_ref[...]
    gram_ref[:half, :half] = left_diag_ref[...]
    gram_ref[:half, half:] = cross
    gram_ref[half:, :half] = cross.T
    gram_ref[half:, half:] = right_diag_ref[...]
    flag = flag_ref[0] == 1
    rotate(gram_ref[...], left_ref[...], right_ref[...], flag, outs)


def rotation_call(body, operands, rows, half, name):
    width = 2 * half
    outs = [
        shape(rows, half),
        shape(width, half),
        shape(half, half),
        shape(half, half),
        shape(1, TILE),
    ]
    specs = [in_smem] + [in_vmem] * (len(operands) - 1)
    scratch = [pltpu.VMEM((width, width), f32)]
    return call(body, outs, specs, 102 * width**3, name, scratch_shapes=scratch)(*operands)


def keep_body(left_ref, right_ref, rot_ref, out_ref):
    rot = split(rot_ref[...])
    half = rot_ref.shape[1]
    top, bottom = tuple(p[:half] for p in rot), tuple(p[half:] for p in rot)
    out_ref[...] = mul(split(left_ref[...]), top) + mul(split(right_ref[...]), bottom)


def kept(left, right, rot):
    rows, half = left.shape
    return call(keep_body, shape(rows, half), [in_vmem] * 3, 12 * rows * half * half, "kept")(left, right, rot)


def join_body(left_ref, right_ref, out_ref):
    half = left_ref.shape[1]
    out_ref[:, :half] = left_ref[...]
    out_ref[:, half:] = right_ref[...]


def from_behind(x):
    count = lax.axis_size("col")
    return lax.ppermute(x, "col", [(i, (i + 1) % count) for i in range(count)])


def sum_over_rows(x):
    count = lax.axis_size("row")
    slices = x.reshape(count, x.shape[0] // count, x.shape[1])
    mine = jnp.sum(lax.all_to_all(slices, "row", 0, 0), axis=0)
    shared = jnp.broadcast_to(mine[None], slices.shape)
    return lax.all_to_all(shared, "row", 0, 0).reshape(x.shape)


def sum_over_pairs(x):
    count = lax.axis_size("col")
    shared = jnp.broadcast_to(x, (count, x.shape[1]))
    return jnp.sum(lax.all_to_all(shared, "col", 0, 0, tiled=True), axis=0)


def on_device(matrix, plan):
    rows, width = matrix.shape
    half = width // 2
    position = lax.axis_index("col")
    flags = lax.dynamic_slice_in_dim(plan, position, 1, axis=1)
    left, right = matrix[:, :half], matrix[:, half:]
    stats = []
    for step in range(STEPS):
        if step == 0:
            gram = sum_over_rows(local_gram(matrix))
            made = rotation_call(first_body, (flags[0], gram, matrix), rows, half, "rotate_first")
        else:
            cross = sum_over_rows(local_cross(left, right))
            operands = (flags[step], left_diag, cross, right_diag, left, right)
            made = rotation_call(later_body, operands, rows, half, "rotate_later")
        send, keep_rot, send_diag, left_diag, stat = made
        stats.append(stat)
        received = from_behind(send)
        if step < STEPS - 1:
            right_diag = from_behind(send_diag)
        left = kept(left, right, keep_rot)
        right = received
    sums = sum_over_pairs(jnp.concatenate(stats, axis=1)).reshape(STEPS, TILE)
    rotated = call(join_body, shape(rows, width), [in_vmem] * 2, 0, "join")(left, right)
    return rotated, jnp.log(sums[:, 0] / sums[:, 1])


def solution(mesh):
    in_specs = (P("row", "col"), P())
    out_specs = (P("row", "col"), P())
    return jax.shard_map(
        on_device, mesh=mesh, in_specs=in_specs, out_specs=out_specs, check_vma=False
    )
```

```python
import functools

import jax
import jax.numpy as jnp
from jax import lax
from jax.experimental import pallas as pl
from jax.experimental.pallas import tpu as pltpu
from jax.sharding import PartitionSpec as P

SWEEPS = 2
STEPS = 3
TILE = 128
VMEM_LIMIT = 24 * 2**20

f32 = jnp.float32
bf16 = jnp.bfloat16
eps = 1e-06
in_smem = pl.BlockSpec(memory_space=pltpu.SMEM)


def split(x):
    high = x.astype(bf16)
    return high, (x - high.astype(f32)).astype(bf16)


def dot(first, second):
    return jnp.dot(first, second, preferred_element_type=f32)


def dot_t(first, second):
    return lax.dot_general(first, second, (((0,), (0,)), ((), ())), preferred_element_type=f32)


def triple(op, first, second):
    return op(first[0], second[0]) + (op(first[0], second[1]) + op(first[1], second[0]))


mul = functools.partial(triple, dot)
mul_t = functools.partial(triple, dot_t)


def columns(parts, start, size):
    return tuple(part[:, start : start + size] for part in parts)


in_any = pl.BlockSpec(memory_space=pl.ANY)
in_hbm = pl.BlockSpec(memory_space=pltpu.HBM)


def call(body, outs, operands, flops, name, scratch=(), flag=None, kept=()):
    single = not isinstance(outs, (list, tuple))
    results = [outs] if single else list(outs)
    count, total = len(operands), len(operands) + len(results)
    skip = 0 if flag is None else 1

    def run(*refs):
        flags, refs = refs[:skip], refs[skip:]
        far, near = refs[:total], refs[total : 2 * total]
        rest, sems = refs[2 * total : -1], refs[-1]
        copies = [pltpu.make_async_copy(far[i], near[i], sems.at[i]) for i in range(count)]
        for copy in copies:
            copy.start()
        for copy in copies:
            copy.wait()
        body(*flags, *near, *rest)
        copies = [pltpu.make_async_copy(near[i], far[i], sems.at[i]) for i in range(count, total)]
        for copy in copies:
            copy.start()
        for copy in copies:
            copy.wait()

    buffers = [pltpu.VMEM(x.shape, f32) for x in (*operands, *results)]
    made = pl.pallas_call(
        run,
        out_shape=results,
        in_specs=[in_smem] * skip + [in_hbm if i in kept else in_any for i in range(count)],
        out_specs=[in_hbm if i in kept else in_any for i in range(count, total)],
        scratch_shapes=[*buffers, *scratch, pltpu.SemaphoreType.DMA((total,))],
        compiler_params=pltpu.CompilerParams(vmem_limit_bytes=VMEM_LIMIT),
        cost_estimate=pl.CostEstimate(flops=flops, bytes_accessed=4 * 2**20, transcendentals=0),
        name=name,
    )(*(() if flag is None else (flag,)), *operands)
    return made[0] if single else made


def shape(*dims):
    return jax.ShapeDtypeStruct(dims, f32)


def tile_pairs(width):
    count = width // TILE
    return [(i, j) for i in range(count) for j in range(i, count)]


def gram_body(pair_ref, out_ref):
    parts = split(pair_ref[...])
    width = pair_ref.shape[1]
    half = width // 2
    blocks = {}
    for i, j in ((0, 0), (0, 1), (1, 1)):
        blocks[i, j] = mul_t(columns(parts, i * half, half), columns(parts, j * half, half))
    per = half // TILE
    for at, (i, j) in enumerate(tile_pairs(width)):
        block = blocks[i // per, j // per]
        r, c = (i % per) * TILE, (j % per) * TILE
        out_ref[at * TILE : (at + 1) * TILE, :] = block[r : r + TILE, c : c + TILE]


def local_gram(pair):
    rows, width = pair.shape
    count = len(tile_pairs(width))
    return call(gram_body, shape(count * TILE, TILE), [pair], 6 * rows * width * width, "local_gram")


def cross_body(mine_ref, ahead_ref, behind_ref, out_ref):
    behind = split(behind_ref[...])
    count, rows, _ = out_ref.shape
    part = rows // 2
    for at, ref in enumerate((mine_ref, ahead_ref)):
        made = mul_t(split(ref[...]), behind)
        for i in range(count):
            out_ref[i, at * part : (at + 1) * part, :] = made[i * part : (i + 1) * part, :]


def local_cross(mine, ahead, behind):
    rows, width = mine.shape
    count = lax.axis_size("row")
    out = shape(count, 2 * width // count, width)
    return call(cross_body, out, [mine, ahead, behind], 12 * rows * width * width, "local_cross")


def share_body(slices_ref, shared_ref, *others):
    count, part, _ = shared_ref.shape
    made = slices_ref[0]
    for i in range(1, count):
        made += slices_ref[i]
    for i in range(count):
        shared_ref[i] = made[:part]
    for ref in others:
        ref[...] = made[part:]


def share(slices):
    return call(share_body, shape(*slices.shape), [slices], slices.size, "share")


def share_first(slices):
    count, rows, width = slices.shape
    outs = [shape(count, rows // 2, width), shape(rows // 2, width)]
    return call(share_body, outs, [slices], slices.size, "share_first")


def apply_body(mine_ref, got_ref, out_ref):
    out_ref[...] = mul(split(mine_ref[...]), split(got_ref[: mine_ref.shape[1], :]))


def apply_got(mine, got):
    out = shape(mine.shape[0], got.shape[1])
    return call(apply_body, out, [mine, got], 6 * mine.size * got.shape[1], "apply_got")


def move_body(left_ref, right_ref, rot_ref, out_ref):
    half = rot_ref.shape[1]
    rot = split(rot_ref[: 2 * half, :])
    top, bottom = tuple(p[:half] for p in rot), tuple(p[half:] for p in rot)
    out_ref[...] = mul(split(left_ref[...]), top) + mul(split(right_ref[...]), bottom)


def move(left, right, rot):
    rows, half = left.shape
    return call(move_body, shape(rows, half), [left, right, rot], 12 * rows * half * half, "move")


def sweep(gram, row, col):
    eye = row == col
    one = eye.astype(f32)
    on_diag = jnp.where(eye, gram, 0.0)
    diag_sum = jnp.sum(on_diag, axis=0, keepdims=True) + jnp.sum(on_diag, axis=1, keepdims=True)
    ratio = gram / (diag_sum + eps)
    skew = jnp.where(col > row, ratio, jnp.where(row > col, -ratio, 0.0))
    norm = jnp.sum(jnp.sum(skew * skew, axis=0, keepdims=True), axis=1, keepdims=True)
    skew = skew * (1.0 / jnp.maximum(jnp.sqrt(norm), 1.0))
    skew_parts = split(skew)
    square = mul(skew_parts, skew_parts)
    t1 = one * (1.0 / 3.0) + square * (2.0 / 3.0)
    t1_parts = split(t1)
    t2 = mul(t1_parts, t1_parts)
    t2_parts = split(t2)
    t4 = mul(t2_parts, t2_parts)
    low = one + t1 + t2 + mul(t1_parts, t2_parts)
    inverse = (low + mul(split(low), split(t4))) * (2.0 / 3.0)
    qmat = mul(split(one - 2.0 * skew + square), split(inverse))
    q_parts = split(qmat)
    return q_parts, mul(split(gram), q_parts)


def rotate(gram, stat_ref):
    width = gram.shape[0]
    half = width // 2
    row = lax.broadcasted_iota(jnp.int32, (width, width), 0)
    col = lax.broadcasted_iota(jnp.int32, (width, width), 1)
    first, half_turned = sweep(gram, row, col)
    gram = mul_t(first, split(half_turned))
    second, half_turned = sweep(gram, row, col)
    rotation = mul(first, second)
    turned = split(half_turned)
    left, right = columns(second, 0, half), columns(second, half, half)
    left_diag = mul_t(left, columns(turned, 0, half))
    right_diag = mul_t(right, columns(turned, half, half))
    cross = mul_t(left, columns(turned, half, half))
    cross_sq = jnp.sum(jnp.sum(cross * cross, axis=0, keepdims=True), axis=1, keepdims=True)
    eye = row[:half, :half] == col[:half, :half]
    on_diag = jnp.where(eye, left_diag * left_diag + right_diag * right_diag, 0.0)
    diag_sq = jnp.sum(jnp.sum(on_diag, axis=0, keepdims=True), axis=1, keepdims=True)
    lane = lax.broadcasted_iota(jnp.int32, stat_ref.shape, 1)
    stat_ref[...] = jnp.where(lane == 0, cross_sq, jnp.where(lane == 1, diag_sq, 0.0))
    return rotation, left_diag, cross, right_diag


def choose(flag, when_right, when_left, ref, at=0):
    ref[at : at + when_right.shape[0], :] = jnp.where(flag, when_right, when_left)


def give(flag, rotation, left_diag, right_diag, pass_ref, keep_ref):
    width = rotation.shape[0]
    half = width // 2
    choose(flag, rotation[:, half:], rotation[:, :half], pass_ref)
    choose(flag, right_diag, left_diag, pass_ref, width)
    choose(flag, rotation[:, :half], rotation[:, half:], keep_ref)
    choose(flag, left_diag, right_diag, keep_ref, width)


def set_gram(gram_ref, left_diag, cross, right_diag):
    half = cross.shape[0]
    gram_ref[:half, :half] = left_diag
    gram_ref[:half, half:] = cross
    gram_ref[half:, :half] = cross.T
    gram_ref[half:, half:] = right_diag


def first_body(flag_ref, tiles_ref, pass_ref, keep_ref, stat_ref, gram_ref):
    for at, (i, j) in enumerate(tile_pairs(gram_ref.shape[0])):
        tile = tiles_ref[at * TILE : (at + 1) * TILE, :]
        gram_ref[i * TILE : (i + 1) * TILE, j * TILE : (j + 1) * TILE] = tile
        if i != j:
            gram_ref[j * TILE : (j + 1) * TILE, i * TILE : (i + 1) * TILE] = tile.T
    flag = flag_ref[0] == 1
    rotation, left_diag, cross, right_diag = rotate(gram_ref[...], stat_ref)
    give(flag, rotation, left_diag, right_diag, pass_ref, keep_ref)
    choose(flag, cross, cross.T, keep_ref, pass_ref.shape[0])


def second_body(flag_ref, mine_keep_ref, mine_pass_ref, got_ref, near_ref, pass_ref, keep_ref, mix_ref, stat_ref, gram_ref):
    width = gram_ref.shape[0]
    half = width // 2
    inner = split(mul(split(near_ref[...]), split(got_ref[:width, :])))
    cross = mul_t(split(mine_keep_ref[:width, :]), inner)
    mix_ref[...] = mul_t(split(mine_pass_ref[:width, :]), inner)
    set_gram(gram_ref, mine_keep_ref[width : width + half, :], cross, got_ref[width:, :])
    flag = flag_ref[0] == 1
    rotation, left_diag, _, right_diag = rotate(gram_ref[...], stat_ref)
    give(flag, rotation, left_diag, right_diag, pass_ref, keep_ref)


def third_body(
    flag_ref, keep1_ref, got1_ref, keep0_ref, far_ref, both_kept_ref, off_ref, mix_ref,
    pass_rot_ref, keep_rot_ref, stat_ref, gram_ref,
):
    width = gram_ref.shape[0]
    half = width // 2
    top, bottom = split(got1_ref[:half, :]), split(got1_ref[half:width, :])
    through = mul(split(far_ref[...]), bottom)
    upper = mul(split(both_kept_ref[...]), top) + mul_t(split(keep0_ref[:width, :]), split(through))
    lower = mul_t(split(off_ref[-half:, :]), top) + mul(split(mix_ref[...]), bottom)
    cross = mul_t(split(keep1_ref[:half, :]), split(upper)) + mul_t(split(keep1_ref[half:width, :]), split(lower))
    set_gram(gram_ref, keep1_ref[width:, :], cross, got1_ref[width:, :])
    flag = flag_ref[0] == 1
    rotation, _, _, _ = rotate(gram_ref[...], stat_ref)
    choose(flag, rotation[:, half:], rotation[:, :half], pass_rot_ref)
    choose(flag, rotation[:, :half], rotation[:, half:], keep_rot_ref)


def rotation_call(body, flag, operands, outs, width, name, kept):
    outs = [shape(*dims) for dims in outs] + [shape(1, TILE)]
    scratch = [pltpu.VMEM((width, width), f32)]
    return call(body, outs, operands, 102 * width**3, name, scratch, flag, kept)


def product(first, second):
    return jnp.dot(first, second, precision=lax.Precision.HIGH, preferred_element_type=f32)


def product_t(first, second):
    dims = (((0,), (0,)), ((), ()))
    return lax.dot_general(first, second, dims, precision=lax.Precision.HIGH, preferred_element_type=f32)


def join_body(left_ref, right_ref, out_ref):
    half = left_ref.shape[1]
    out_ref[:, :half] = left_ref[...]
    out_ref[:, half:] = right_ref[...]


def from_behind(x, by=1):
    count = lax.axis_size("col")
    return lax.ppermute(x, "col", [(i, (i + by) % count) for i in range(count)])


def swap_rows(slices):
    return lax.all_to_all(slices, "row", 0, 0)


def flat(slices):
    return slices.reshape(slices.shape[0] * slices.shape[1], slices.shape[2])


def gather_rows(mine):
    count = lax.axis_size("row")
    return flat(swap_rows(jnp.broadcast_to(mine[None], (count, *mine.shape))))


def sum_over_pairs(x):
    count = lax.axis_size("col")
    shared = jnp.broadcast_to(x, (count, x.shape[1]))
    return jnp.sum(lax.all_to_all(shared, "col", 0, 0, tiled=True), axis=0)


def after(x, *others):
    return lax.optimization_barrier((x, *others))[0]


def on_device(matrix, plan):
    rows, width = matrix.shape
    half = width // 2
    stacked = (width + half, half)
    position = lax.axis_index("col")
    flags = lax.dynamic_slice_in_dim(plan, position, 1, axis=1)

    behind = from_behind(matrix)
    ahead = from_behind(matrix, -1)
    tiles = local_gram(matrix)
    count = lax.axis_size("row")
    slices = swap_rows(tiles.reshape(count, tiles.shape[0] // count, TILE))
    gram = flat(swap_rows(share(slices)))
    slices = swap_rows(local_cross(matrix, ahead, behind))

    outs = (stacked, (2 * width, half))
    mine_pass, mine_keep, stat0 = rotation_call(first_body, flags[0], (gram,), outs, width, "rotate_first", (1, 2))
    got = from_behind(mine_pass)
    near_shared, far_mine = share_first(after(slices, mine_pass))
    near = flat(swap_rows(near_shared))
    left = product(matrix, after(mine_keep, near_shared)[:width])
    far_mine = apply_got(far_mine, got)
    got_keep = from_behind(after(mine_keep, far_mine))
    far_mine = from_behind(far_mine)

    operands = (mine_keep, mine_pass, got, near)
    outs = (stacked, stacked, (half, half))
    next_pass, next_keep, mix, stat1 = rotation_call(second_body, flags[1], operands, outs, width, "rotate_second", (0, 1, 4, 5, 6))
    next_got = from_behind(next_pass)
    far = gather_rows(after(far_mine, next_pass))
    got_mix = from_behind(after(mix, next_pass))
    first_keep, first_got = after(mine_keep, next_pass), after(got, next_pass)
    right = product(behind, first_got[:width])
    received = from_behind(after(move(left, right, next_pass), next_got))
    both_kept = product_t(first_keep[:width], product(near, got_keep[:width]))

    operands = (next_keep, next_got, mine_keep, far, both_kept, got_keep, got_mix)
    outs = ((width, half), (width, half))
    pass_rot, keep_rot, stat2 = rotation_call(third_body, flags[2], operands, outs, width, "rotate_third", (0, 2))
    left = move(left, right, next_keep)
    moved = move(left, received, pass_rot)
    last = from_behind(moved)
    left = move(left, received, after(keep_rot, moved))
    stats, left = lax.optimization_barrier((jnp.concatenate([stat0, stat1, stat2], axis=1), left))
    sums = sum_over_pairs(stats).reshape(STEPS, TILE)
    rotated = call(join_body, shape(rows, width), [left, last], 0, "join")
    return rotated, jnp.log(sums[:, 0] / sums[:, 1])


def solution(mesh):
    in_specs = (P("row", "col"), P())
    out_specs = (P("row", "col"), P())
    return jax.shard_map(
        on_device, mesh=mesh, in_specs=in_specs, out_specs=out_specs, check_vma=False
    )
```

```python
import functools

import jax
import jax.numpy as jnp
from jax import lax
from jax.experimental import pallas as pl
from jax.experimental.pallas import tpu as pltpu
from jax.sharding import PartitionSpec as P

SWEEPS = 2
STEPS = 3
SHARE_FLOPS = 2 * 10**10
TILE = 128
VMEM_LIMIT = 24 * 2**20

f32 = jnp.float32
bf16 = jnp.bfloat16
eps = 1e-06
in_smem = pl.BlockSpec(memory_space=pltpu.SMEM)
in_vmem = pl.BlockSpec(memory_space=pltpu.VMEM)


def split(x):
    high = x.astype(bf16)
    return high, (x - high.astype(f32)).astype(bf16)


def dot(first, second):
    return jnp.dot(first, second, preferred_element_type=f32)


def dot_t(first, second):
    return lax.dot_general(first, second, (((0,), (0,)), ((), ())), preferred_element_type=f32)


def triple(op, first, second):
    return op(first[0], second[0]) + (op(first[0], second[1]) + op(first[1], second[0]))


mul = functools.partial(triple, dot)
mul_t = functools.partial(triple, dot_t)


def columns(parts, start, size):
    return tuple(part[:, start : start + size] for part in parts)


in_any = pl.BlockSpec(memory_space=pl.ANY)
in_hbm = pl.BlockSpec(memory_space=pltpu.HBM)


def call(body, outs, operands, flops, name, scratch=(), flag=None, kept=()):
    single = not isinstance(outs, (list, tuple))
    results = [outs] if single else list(outs)
    count, total = len(operands), len(operands) + len(results)
    skip = 0 if flag is None else 1

    def run(*refs):
        flags, refs = refs[:skip], refs[skip:]
        far, near = refs[:total], refs[total : 2 * total]
        rest, sems = refs[2 * total : -1], refs[-1]
        copies = [pltpu.make_async_copy(far[i], near[i], sems.at[i]) for i in range(count)]
        for copy in copies:
            copy.start()
        for copy in copies:
            copy.wait()
        body(*flags, *near, *rest)
        copies = [pltpu.make_async_copy(near[i], far[i], sems.at[i]) for i in range(count, total)]
        for copy in copies:
            copy.start()
        for copy in copies:
            copy.wait()

    buffers = [pltpu.VMEM(x.shape, f32) for x in (*operands, *results)]
    made = pl.pallas_call(
        run,
        out_shape=results,
        in_specs=[in_smem] * skip + [in_hbm if i in kept else in_any for i in range(count)],
        out_specs=[in_hbm if i in kept else in_any for i in range(count, total)],
        scratch_shapes=[*buffers, *scratch, pltpu.SemaphoreType.DMA((total,))],
        compiler_params=pltpu.CompilerParams(vmem_limit_bytes=VMEM_LIMIT),
        cost_estimate=pl.CostEstimate(flops=flops, bytes_accessed=4 * 2**20, transcendentals=0),
        name=name,
    )(*(() if flag is None else (flag,)), *operands)
    return made[0] if single else made


def shape(*dims):
    return jax.ShapeDtypeStruct(dims, f32)


def tile_pairs(width):
    count = width // TILE
    return [(i, j) for i in range(count) for j in range(i, count)]


def gram_body(pair_ref, out_ref):
    parts = split(pair_ref[...])
    width = pair_ref.shape[1]
    half = width // 2
    blocks = {}
    for i, j in ((0, 0), (0, 1), (1, 1)):
        blocks[i, j] = mul_t(columns(parts, i * half, half), columns(parts, j * half, half))
    per = half // TILE
    for at, (i, j) in enumerate(tile_pairs(width)):
        block = blocks[i // per, j // per]
        r, c = (i % per) * TILE, (j % per) * TILE
        out_ref[at * TILE : (at + 1) * TILE, :] = block[r : r + TILE, c : c + TILE]


def local_gram(pair):
    rows, width = pair.shape
    count = len(tile_pairs(width))
    return call(gram_body, shape(count * TILE, TILE), [pair], 6 * rows * width * width, "local_gram")


def cross_body(mine_ref, ahead_ref, behind_ref, out_ref):
    behind = split(behind_ref[...])
    count, rows, _ = out_ref.shape
    part = rows // 2
    for at, ref in enumerate((mine_ref, ahead_ref)):
        made = mul_t(split(ref[...]), behind)
        for i in range(count):
            out_ref[i, at * part : (at + 1) * part, :] = made[i * part : (i + 1) * part, :]


def local_cross(mine, ahead, behind):
    rows, width = mine.shape
    count = lax.axis_size("row")
    out = shape(count, 2 * width // count, width)
    return call(cross_body, out, [mine, ahead, behind], 12 * rows * width * width, "local_cross")


def share_body(slices_ref, shared_ref, *others):
    count, part, _ = shared_ref.shape
    made = slices_ref[0]
    for i in range(1, count):
        made += slices_ref[i]
    for i in range(count):
        shared_ref[i] = made[:part]
    for ref in others:
        ref[...] = made[part:]


def share(slices, flops):
    return call(share_body, shape(*slices.shape), [slices], flops, "share")


def share_first(slices):
    count, rows, width = slices.shape
    outs = [shape(count, rows // 2, width), shape(rows // 2, width)]
    return call(share_body, outs, [slices], slices.size, "share_first")


def apply_body(mine_ref, got_ref, out_ref):
    out_ref[...] = mul(split(mine_ref[...]), split(got_ref[: mine_ref.shape[1], :]))


def apply_got(mine, got):
    out = shape(mine.shape[0], got.shape[1])
    return call(apply_body, out, [mine, got], 6 * mine.size * got.shape[1], "apply_got")


def move_body(left_ref, right_ref, rot_ref, out_ref):
    half = rot_ref.shape[1]
    rot = split(rot_ref[: 2 * half, :])
    top, bottom = tuple(p[:half] for p in rot), tuple(p[half:] for p in rot)
    out_ref[...] = mul(split(left_ref[...]), top) + mul(split(right_ref[...]), bottom)


def move(left, right, rot):
    rows, half = left.shape
    return call(move_body, shape(rows, half), [left, right, rot], 12 * rows * half * half, "move")


def squared(parts):
    mixed = dot(parts[0], parts[1])
    return dot(parts[0], parts[0]) + (mixed + mixed.T)


def sweep(gram, row, col):
    eye = row == col
    one = eye.astype(f32)
    on_diag = jnp.where(eye, gram, 0.0)
    diag_sum = jnp.sum(on_diag, axis=0, keepdims=True) + jnp.sum(on_diag, axis=1, keepdims=True)
    ratio = gram / (diag_sum + eps)
    skew = jnp.where(col > row, ratio, jnp.where(row > col, -ratio, 0.0))
    norm = jnp.sum(jnp.sum(skew * skew, axis=0, keepdims=True), axis=1, keepdims=True)
    skew = skew * (1.0 / jnp.maximum(jnp.sqrt(norm), 1.0))
    skew_parts = split(skew)
    square = squared(skew_parts)
    square_parts = split(square)
    fourth = squared(square_parts)
    cube = mul(skew_parts, square_parts)
    low = one * (8.0 / 9.0) + (2.0 * fourth + 6.0 * square - 8.0 * skew - 4.0 * cube) * (2.0 / 9.0)
    z = (square + fourth) * (4.0 / 9.0)
    z_short = z.astype(bf16)
    y = z * (2.0 / 9.0) + dot(z_short, z_short)
    high = one * (820.0 / 729.0) + z * (82.0 / 81.0) + y * (10.0 / 9.0) + dot(z_short, y.astype(bf16))
    q_parts = split(mul(split(low), split(high)))
    return q_parts, mul(split(gram), q_parts)


def rotate(gram, stat_ref):
    width = gram.shape[0]
    half = width // 2
    row = lax.broadcasted_iota(jnp.int32, (width, width), 0)
    col = lax.broadcasted_iota(jnp.int32, (width, width), 1)
    first, half_turned = sweep(gram, row, col)
    gram = mul_t(first, split(half_turned))
    second, half_turned = sweep(gram, row, col)
    rotation = mul(first, second)
    turned = split(half_turned)
    left, right = columns(second, 0, half), columns(second, half, half)
    left_diag = mul_t(left, columns(turned, 0, half))
    right_diag = mul_t(right, columns(turned, half, half))
    cross = mul_t(left, columns(turned, half, half))
    cross_sq = jnp.sum(jnp.sum(cross * cross, axis=0, keepdims=True), axis=1, keepdims=True)
    eye = row[:half, :half] == col[:half, :half]
    on_diag = jnp.where(eye, left_diag * left_diag + right_diag * right_diag, 0.0)
    diag_sq = jnp.sum(jnp.sum(on_diag, axis=0, keepdims=True), axis=1, keepdims=True)
    lane = lax.broadcasted_iota(jnp.int32, stat_ref.shape, 1)
    stat_ref[...] = jnp.where(lane == 0, cross_sq, jnp.where(lane == 1, diag_sq, 0.0))
    return rotation, left_diag, cross, right_diag


def choose(flag, when_right, when_left, ref, at=0):
    ref[at : at + when_right.shape[0], :] = jnp.where(flag, when_right, when_left)


def give(flag, rotation, left_diag, right_diag, pass_ref, keep_ref):
    width = rotation.shape[0]
    half = width // 2
    choose(flag, rotation[:, half:], rotation[:, :half], pass_ref)
    choose(flag, right_diag, left_diag, pass_ref, width)
    choose(flag, rotation[:, :half], rotation[:, half:], keep_ref)
    choose(flag, left_diag, right_diag, keep_ref, width)


def set_gram(gram_ref, left_diag, cross, right_diag):
    half = cross.shape[0]
    gram_ref[:half, :half] = left_diag
    gram_ref[:half, half:] = cross
    gram_ref[half:, :half] = cross.T
    gram_ref[half:, half:] = right_diag


def first_body(flag_ref, tiles_ref, pass_ref, keep_ref, stat_ref, gram_ref):
    for at, (i, j) in enumerate(tile_pairs(gram_ref.shape[0])):
        tile = tiles_ref[at * TILE : (at + 1) * TILE, :]
        gram_ref[i * TILE : (i + 1) * TILE, j * TILE : (j + 1) * TILE] = tile
        if i != j:
            gram_ref[j * TILE : (j + 1) * TILE, i * TILE : (i + 1) * TILE] = tile.T
    flag = flag_ref[0] == 1
    rotation, left_diag, cross, right_diag = rotate(gram_ref[...], stat_ref)
    give(flag, rotation, left_diag, right_diag, pass_ref, keep_ref)
    choose(flag, cross, cross.T, keep_ref, pass_ref.shape[0])


def second_body(flag_ref, mine_keep_ref, mine_pass_ref, got_ref, near_ref, pass_ref, keep_ref, mix_ref, stat_ref, gram_ref):
    width = gram_ref.shape[0]
    half = width // 2
    inner = split(mul(split(near_ref[...]), split(got_ref[:width, :])))
    cross = mul_t(split(mine_keep_ref[:width, :]), inner)
    mix_ref[...] = mul_t(split(mine_pass_ref[:width, :]), inner)
    set_gram(gram_ref, mine_keep_ref[width : width + half, :], cross, got_ref[width:, :])
    flag = flag_ref[0] == 1
    rotation, left_diag, _, right_diag = rotate(gram_ref[...], stat_ref)
    give(flag, rotation, left_diag, right_diag, pass_ref, keep_ref)


def third_body(
    flag_ref, keep1_ref, got1_ref, keep0_ref, far_ref, both_kept_ref, off_ref, mix_ref,
    pass_rot_ref, keep_rot_ref, stat_ref, gram_ref,
):
    width = gram_ref.shape[0]
    half = width // 2
    top, bottom = split(got1_ref[:half, :]), split(got1_ref[half:width, :])
    through = mul(split(far_ref[...]), bottom)
    upper = mul(split(both_kept_ref[...]), top) + mul_t(split(keep0_ref[:width, :]), split(through))
    lower = mul_t(split(off_ref[-half:, :]), top) + mul(split(mix_ref[...]), bottom)
    cross = mul_t(split(keep1_ref[:half, :]), split(upper)) + mul_t(split(keep1_ref[half:width, :]), split(lower))
    set_gram(gram_ref, keep1_ref[width:, :], cross, got1_ref[width:, :])
    flag = flag_ref[0] == 1
    rotation, _, _, _ = rotate(gram_ref[...], stat_ref)
    choose(flag, rotation[:, half:], rotation[:, :half], pass_rot_ref)
    choose(flag, rotation[:, :half], rotation[:, half:], keep_rot_ref)


def rotation_call(body, flag, operands, outs, width, name, kept):
    outs = [shape(*dims) for dims in outs] + [shape(1, TILE)]
    scratch = [pltpu.VMEM((width, width), f32)]
    return call(body, outs, operands, 88 * width**3, name, scratch, flag, kept)


def product(first, second):
    return jnp.dot(first, second, precision=lax.Precision.HIGH, preferred_element_type=f32)


def product_t(first, second):
    dims = (((0,), (0,)), ((), ()))
    return lax.dot_general(first, second, dims, precision=lax.Precision.HIGH, preferred_element_type=f32)


def join_body(left_ref, right_ref, out_ref):
    half = left_ref.shape[1]
    out_ref[:, :half] = left_ref[...]
    out_ref[:, half:] = right_ref[...]


def join(left, right):
    rows, half = left.shape
    out = shape(rows, 2 * half)
    return pl.pallas_call(join_body, out_shape=out, in_specs=[in_vmem] * 2, out_specs=in_vmem, name="join")(left, right)


def from_behind(x, by=1):
    count = lax.axis_size("col")
    return lax.ppermute(x, "col", [(i, (i + by) % count) for i in range(count)])


def swap_rows(slices):
    return lax.all_to_all(slices, "row", 0, 0)


def flat(slices):
    return slices.reshape(slices.shape[0] * slices.shape[1], slices.shape[2])


def gather_rows(mine):
    count = lax.axis_size("row")
    return flat(swap_rows(jnp.broadcast_to(mine[None], (count, *mine.shape))))


def sum_over_pairs(x):
    count = lax.axis_size("col")
    shared = jnp.broadcast_to(x, (count, x.shape[1]))
    return jnp.sum(lax.all_to_all(shared, "col", 0, 0, tiled=True), axis=0)


def after(x, *others):
    return lax.optimization_barrier((x, *others))[0]


def on_device(matrix, plan):
    rows, width = matrix.shape
    half = width // 2
    stacked = (width + half, half)
    position = lax.axis_index("col")
    flags = lax.dynamic_slice_in_dim(plan, position, 1, axis=1)

    behind = from_behind(matrix)
    ahead = from_behind(matrix, -1)
    tiles = local_gram(matrix)
    count = lax.axis_size("row")
    slices = swap_rows(tiles.reshape(count, tiles.shape[0] // count, TILE))
    gram = flat(swap_rows(share(slices, SHARE_FLOPS)))
    slices = swap_rows(local_cross(matrix, ahead, behind))

    outs = (stacked, (2 * width, half))
    mine_pass, mine_keep, stat0 = rotation_call(first_body, flags[0], (gram,), outs, width, "rotate_first", (1, 2))
    got = from_behind(mine_pass)
    near_shared, far_mine = share_first(after(slices, mine_pass))
    near = flat(swap_rows(near_shared))
    left = product(matrix, after(mine_keep, near_shared)[:width])
    far_mine = apply_got(far_mine, got)
    got_keep = from_behind(after(mine_keep, far_mine))
    far_mine = from_behind(far_mine)

    operands = (mine_keep, mine_pass, got, near)
    outs = (stacked, stacked, (half, half))
    next_pass, next_keep, mix, stat1 = rotation_call(second_body, flags[1], operands, outs, width, "rotate_second", (0, 1, 4, 5, 6))
    next_got = from_behind(next_pass)
    far = gather_rows(after(far_mine, next_pass))
    got_mix = from_behind(after(mix, next_pass))
    first_keep, first_got = after(mine_keep, next_pass), after(got, next_pass)
    right = product(behind, first_got[:width])
    received = from_behind(after(move(left, right, next_pass), next_got))
    both_kept = product_t(first_keep[:width], product(near, got_keep[:width]))

    operands = (next_keep, next_got, mine_keep, far, both_kept, got_keep, got_mix)
    outs = ((width, half), (width, half))
    pass_rot, keep_rot, stat2 = rotation_call(third_body, flags[2], operands, outs, width, "rotate_third", (0, 2))
    left = move(left, right, next_keep)
    moved = move(left, received, pass_rot)
    last = from_behind(moved)
    left = move(left, received, after(keep_rot, moved))
    stats, left = lax.optimization_barrier((jnp.concatenate([stat0, stat1, stat2], axis=1), left))
    sums = sum_over_pairs(stats).reshape(STEPS, TILE)
    rotated = join(left, last)
    return rotated, jnp.log(sums[:, 0] / sums[:, 1])


def solution(mesh):
    in_specs = (P("row", "col"), P())
    out_specs = (P("row", "col"), P())
    return jax.shard_map(
        on_device, mesh=mesh, in_specs=in_specs, out_specs=out_specs, check_vma=False
    )
```

```python
import functools

import jax
import jax.numpy as jnp
from jax import lax
from jax.experimental import pallas as pl
from jax.experimental.pallas import tpu as pltpu
from jax.sharding import PartitionSpec as P

SWEEPS = 2
STEPS = 3
SHARE_FLOPS = 2 * 10**10
EARLY_FLOPS = 2 * 10**9
TILE = 128
VMEM_LIMIT = 24 * 2**20

f32 = jnp.float32
bf16 = jnp.bfloat16
eps = 1e-06
in_smem = pl.BlockSpec(memory_space=pltpu.SMEM)


def split(x):
    high = x.astype(bf16)
    return high, (x - high.astype(f32)).astype(bf16)


def dot(first, second):
    return jnp.dot(first, second, preferred_element_type=f32)


def dot_t(first, second):
    return lax.dot_general(first, second, (((0,), (0,)), ((), ())), preferred_element_type=f32)


def triple(op, first, second):
    return op(first[0], second[0]) + (op(first[0], second[1]) + op(first[1], second[0]))


mul = functools.partial(triple, dot)
mul_t = functools.partial(triple, dot_t)


def columns(parts, start, size):
    return tuple(part[:, start : start + size] for part in parts)


in_any = pl.BlockSpec(memory_space=pl.ANY)
in_hbm = pl.BlockSpec(memory_space=pltpu.HBM)


def call(body, outs, operands, flops, name, scratch=(), flag=None, kept=()):
    single = not isinstance(outs, (list, tuple))
    results = [outs] if single else list(outs)
    count, total = len(operands), len(operands) + len(results)
    skip = 0 if flag is None else 1

    def run(*refs):
        flags, refs = refs[:skip], refs[skip:]
        far, near = refs[:total], refs[total : 2 * total]
        rest, sems = refs[2 * total : -1], refs[-1]
        copies = [pltpu.make_async_copy(far[i], near[i], sems.at[i]) for i in range(count)]
        for copy in copies:
            copy.start()
        for copy in copies:
            copy.wait()
        body(*flags, *near, *rest)
        copies = [pltpu.make_async_copy(near[i], far[i], sems.at[i]) for i in range(count, total)]
        for copy in copies:
            copy.start()
        for copy in copies:
            copy.wait()

    buffers = [pltpu.VMEM(x.shape, f32) for x in (*operands, *results)]
    made = pl.pallas_call(
        run,
        out_shape=results,
        in_specs=[in_smem] * skip + [in_hbm if i in kept else in_any for i in range(count)],
        out_specs=[in_hbm if i in kept else in_any for i in range(count, total)],
        scratch_shapes=[*buffers, *scratch, pltpu.SemaphoreType.DMA((total,))],
        compiler_params=pltpu.CompilerParams(vmem_limit_bytes=VMEM_LIMIT),
        cost_estimate=pl.CostEstimate(flops=flops, bytes_accessed=4 * 2**20, transcendentals=0),
        name=name,
    )(*(() if flag is None else (flag,)), *operands)
    return made[0] if single else made


def shape(*dims):
    return jax.ShapeDtypeStruct(dims, f32)


def tile_pairs(width):
    count = width // TILE
    return [(i, j) for i in range(count) for j in range(i, count)]


def gram_body(pair_ref, out_ref):
    parts = split(pair_ref[...])
    width = pair_ref.shape[1]
    half = width // 2
    blocks = {}
    for i, j in ((0, 0), (0, 1), (1, 1)):
        blocks[i, j] = mul_t(columns(parts, i * half, half), columns(parts, j * half, half))
    per = half // TILE
    for at, (i, j) in enumerate(tile_pairs(width)):
        block = blocks[i // per, j // per]
        r, c = (i % per) * TILE, (j % per) * TILE
        out_ref[at * TILE : (at + 1) * TILE, :] = block[r : r + TILE, c : c + TILE]


def local_gram(pair):
    rows, width = pair.shape
    count = len(tile_pairs(width))
    return call(gram_body, shape(count * TILE, TILE), [pair], 6 * rows * width * width, "local_gram")


def cross_body(mine_ref, ahead_ref, behind_ref, out_ref):
    behind = split(behind_ref[...])
    count, rows, _ = out_ref.shape
    part = rows // 2
    for at, ref in enumerate((mine_ref, ahead_ref)):
        made = mul_t(split(ref[...]), behind)
        for i in range(count):
            out_ref[i, at * part : (at + 1) * part, :] = made[i * part : (i + 1) * part, :]


def local_cross(mine, ahead, behind):
    rows, width = mine.shape
    count = lax.axis_size("row")
    out = shape(count, 2 * width // count, width)
    return call(cross_body, out, [mine, ahead, behind], 12 * rows * width * width, "local_cross")


def share_body(slices_ref, shared_ref, *others):
    count, part, _ = shared_ref.shape
    made = slices_ref[0]
    for i in range(1, count):
        made += slices_ref[i]
    for i in range(count):
        shared_ref[i] = made[:part]
    for ref in others:
        ref[...] = made[part:]


def share(slices, flops):
    return call(share_body, shape(*slices.shape), [slices], flops, "share")


def share_first(slices):
    count, rows, width = slices.shape
    outs = [shape(count, rows // 2, width), shape(rows // 2, width)]
    return call(share_body, outs, [slices], slices.size, "share_first")


def apply_body(mine_ref, got_ref, out_ref):
    out_ref[...] = mul(split(mine_ref[...]), split(got_ref[: mine_ref.shape[1], :]))


def apply_got(mine, got):
    out = shape(mine.shape[0], got.shape[1])
    return call(apply_body, out, [mine, got], EARLY_FLOPS, "apply_got")


def move_body(left_ref, right_ref, rot_ref, out_ref):
    half = rot_ref.shape[1]
    rot = split(rot_ref[: 2 * half, :])
    top, bottom = tuple(p[:half] for p in rot), tuple(p[half:] for p in rot)
    out_ref[...] = mul(split(left_ref[...]), top) + mul(split(right_ref[...]), bottom)


def move(left, right, rot):
    rows, half = left.shape
    return call(move_body, shape(rows, half), [left, right, rot], 12 * rows * half * half, "move")


def squared(parts):
    mixed = dot(parts[0], parts[1])
    return dot(parts[0], parts[0]) + (mixed + mixed.T)


def sweep(gram, row, col):
    eye = row == col
    one = eye.astype(f32)
    on_diag = jnp.where(eye, gram, 0.0)
    diag_sum = jnp.sum(on_diag, axis=0, keepdims=True) + jnp.sum(on_diag, axis=1, keepdims=True)
    ratio = gram / (diag_sum + eps)
    skew = jnp.where(col > row, ratio, jnp.where(row > col, -ratio, 0.0))
    norm = jnp.sum(jnp.sum(skew * skew, axis=0, keepdims=True), axis=1, keepdims=True)
    skew = skew * (1.0 / jnp.maximum(jnp.sqrt(norm), 1.0))
    skew_parts = split(skew)
    square = squared(skew_parts)
    square_parts = split(square)
    fourth = squared(square_parts)
    cube = mul(skew_parts, square_parts)
    low = one * (8.0 / 9.0) + (2.0 * fourth + 6.0 * square - 8.0 * skew - 4.0 * cube) * (2.0 / 9.0)
    z = (square + fourth) * (4.0 / 9.0)
    z_short = z.astype(bf16)
    y = z * (2.0 / 9.0) + dot(z_short, z_short)
    high = one * (820.0 / 729.0) + z * (82.0 / 81.0) + y * (10.0 / 9.0) + dot(z_short, y.astype(bf16))
    q_parts = split(mul(split(low), split(high)))
    return q_parts, mul(split(gram), q_parts)


def rotate(gram, stat_ref):
    width = gram.shape[0]
    half = width // 2
    row = lax.broadcasted_iota(jnp.int32, (width, width), 0)
    col = lax.broadcasted_iota(jnp.int32, (width, width), 1)
    first, half_turned = sweep(gram, row, col)
    gram = mul_t(first, split(half_turned))
    second, half_turned = sweep(gram, row, col)
    rotation = mul(first, second)
    turned = split(half_turned)
    left, right = columns(second, 0, half), columns(second, half, half)
    left_diag = mul_t(left, columns(turned, 0, half))
    right_diag = mul_t(right, columns(turned, half, half))
    cross = mul_t(left, columns(turned, half, half))
    cross_sq = jnp.sum(jnp.sum(cross * cross, axis=0, keepdims=True), axis=1, keepdims=True)
    eye = row[:half, :half] == col[:half, :half]
    on_diag = jnp.where(eye, left_diag * left_diag + right_diag * right_diag, 0.0)
    diag_sq = jnp.sum(jnp.sum(on_diag, axis=0, keepdims=True), axis=1, keepdims=True)
    lane = lax.broadcasted_iota(jnp.int32, stat_ref.shape, 1)
    stat_ref[...] = jnp.where(lane == 0, cross_sq, jnp.where(lane == 1, diag_sq, 0.0))
    return rotation, left_diag, cross, right_diag


def choose(flag, when_right, when_left, ref, at=0):
    ref[at : at + when_right.shape[0], :] = jnp.where(flag, when_right, when_left)


def give(flag, rotation, left_diag, right_diag, pass_ref, keep_ref):
    width = rotation.shape[0]
    half = width // 2
    choose(flag, rotation[:, half:], rotation[:, :half], pass_ref)
    choose(flag, right_diag, left_diag, pass_ref, width)
    choose(flag, rotation[:, :half], rotation[:, half:], keep_ref)
    choose(flag, left_diag, right_diag, keep_ref, width)


def set_gram(gram_ref, left_diag, cross, right_diag):
    half = cross.shape[0]
    gram_ref[:half, :half] = left_diag
    gram_ref[:half, half:] = cross
    gram_ref[half:, :half] = cross.T
    gram_ref[half:, half:] = right_diag


def first_body(flag_ref, tiles_ref, pass_ref, keep_ref, stat_ref, gram_ref):
    for at, (i, j) in enumerate(tile_pairs(gram_ref.shape[0])):
        tile = tiles_ref[at * TILE : (at + 1) * TILE, :]
        gram_ref[i * TILE : (i + 1) * TILE, j * TILE : (j + 1) * TILE] = tile
        if i != j:
            gram_ref[j * TILE : (j + 1) * TILE, i * TILE : (i + 1) * TILE] = tile.T
    flag = flag_ref[0] == 1
    rotation, left_diag, cross, right_diag = rotate(gram_ref[...], stat_ref)
    give(flag, rotation, left_diag, right_diag, pass_ref, keep_ref)
    choose(flag, cross, cross.T, keep_ref, pass_ref.shape[0])


def second_body(flag_ref, mine_keep_ref, mine_pass_ref, got_ref, near_ref, pass_ref, keep_ref, mix_ref, stat_ref, gram_ref):
    width = gram_ref.shape[0]
    half = width // 2
    inner = split(mul(split(near_ref[...]), split(got_ref[:width, :])))
    cross = mul_t(split(mine_keep_ref[:width, :]), inner)
    mix_ref[...] = mul_t(split(mine_pass_ref[:width, :]), inner)
    set_gram(gram_ref, mine_keep_ref[width : width + half, :], cross, got_ref[width:, :])
    flag = flag_ref[0] == 1
    rotation, left_diag, _, right_diag = rotate(gram_ref[...], stat_ref)
    give(flag, rotation, left_diag, right_diag, pass_ref, keep_ref)


def third_body(
    flag_ref, keep1_ref, got1_ref, keep0_ref, far_ref, both_kept_ref, off_ref, mix_ref,
    pass_rot_ref, keep_rot_ref, stat_ref, gram_ref,
):
    width = gram_ref.shape[0]
    half = width // 2
    top, bottom = split(got1_ref[:half, :]), split(got1_ref[half:width, :])
    through = mul(split(far_ref[...]), bottom)
    upper = mul(split(both_kept_ref[...]), top) + mul_t(split(keep0_ref[:width, :]), split(through))
    lower = mul_t(split(off_ref[-half:, :]), top) + mul(split(mix_ref[...]), bottom)
    cross = mul_t(split(keep1_ref[:half, :]), split(upper)) + mul_t(split(keep1_ref[half:width, :]), split(lower))
    set_gram(gram_ref, keep1_ref[width:, :], cross, got1_ref[width:, :])
    flag = flag_ref[0] == 1
    rotation, _, _, _ = rotate(gram_ref[...], stat_ref)
    choose(flag, rotation[:, half:], rotation[:, :half], pass_rot_ref)
    choose(flag, rotation[:, :half], rotation[:, half:], keep_rot_ref)


def rotation_call(body, flag, operands, outs, width, name, kept):
    outs = [shape(*dims) for dims in outs] + [shape(1, TILE)]
    scratch = [pltpu.VMEM((width, width), f32)]
    return call(body, outs, operands, 88 * width**3, name, scratch, flag, kept)


def product(first, second):
    return jnp.dot(first, second, precision=lax.Precision.HIGH, preferred_element_type=f32)


def product_t(first, second):
    dims = (((0,), (0,)), ((), ()))
    return lax.dot_general(first, second, dims, precision=lax.Precision.HIGH, preferred_element_type=f32)


def left_body(left_ref, right_ref, rot_ref, out_ref, left, right, rot, made, sems):
    copies = [
        pltpu.make_async_copy(far, near, sems.at[i])
        for i, (far, near) in enumerate(((left_ref, left), (right_ref, right), (rot_ref, rot)))
    ]
    for copy in copies:
        copy.start()
    for copy in copies:
        copy.wait()
    move_body(left, right, rot, made)
    copy = pltpu.make_async_copy(made, out_ref.at[:, : made.shape[1]], sems.at[3])
    copy.start()
    copy.wait()


def left_half(left, right, rot):
    rows, half = left.shape
    buffers = [pltpu.VMEM(x.shape, f32) for x in (left, right, rot, left)]
    return pl.pallas_call(
        left_body,
        out_shape=shape(rows, 2 * half),
        in_specs=[in_any] * 3,
        out_specs=in_any,
        scratch_shapes=[*buffers, pltpu.SemaphoreType.DMA((4,))],
        compiler_params=pltpu.CompilerParams(vmem_limit_bytes=VMEM_LIMIT),
        name="left_half",
    )(left, right, rot)


def join_body(part_ref, right_ref, out_ref, right, sems):
    copy = pltpu.make_async_copy(right_ref, right, sems.at[0])
    copy.start()
    copy.wait()
    copy = pltpu.make_async_copy(right, out_ref.at[:, right.shape[1] :], sems.at[1])
    copy.start()
    copy.wait()


def join(part, right):
    return pl.pallas_call(
        join_body,
        out_shape=shape(*part.shape),
        in_specs=[in_any] * 2,
        out_specs=in_any,
        scratch_shapes=[pltpu.VMEM(right.shape, f32), pltpu.SemaphoreType.DMA((2,))],
        input_output_aliases={0: 0},
        name="join",
    )(part, right)


def from_behind(x, by=1):
    count = lax.axis_size("col")
    return lax.ppermute(x, "col", [(i, (i + by) % count) for i in range(count)])


def swap_rows(slices):
    return lax.all_to_all(slices, "row", 0, 0)


def flat(slices):
    return slices.reshape(slices.shape[0] * slices.shape[1], slices.shape[2])


def gather_rows(mine):
    count = lax.axis_size("row")
    return flat(swap_rows(jnp.broadcast_to(mine[None], (count, *mine.shape))))


def sum_over_pairs(x):
    count = lax.axis_size("col")
    shared = jnp.broadcast_to(x, (count, x.shape[1]))
    return jnp.sum(lax.all_to_all(shared, "col", 0, 0, tiled=True), axis=0)


def after(x, *others):
    return lax.optimization_barrier((x, *others))[0]


def on_device(matrix, plan):
    rows, width = matrix.shape
    half = width // 2
    stacked = (width + half, half)
    position = lax.axis_index("col")
    flags = lax.dynamic_slice_in_dim(plan, position, 1, axis=1)

    behind = from_behind(matrix)
    ahead = from_behind(matrix, -1)
    tiles = local_gram(matrix)
    count = lax.axis_size("row")
    slices = swap_rows(tiles.reshape(count, tiles.shape[0] // count, TILE))
    gram = flat(swap_rows(share(slices, SHARE_FLOPS)))
    slices = swap_rows(local_cross(matrix, ahead, behind))

    outs = (stacked, (2 * width, half))
    mine_pass, mine_keep, stat0 = rotation_call(first_body, flags[0], (gram,), outs, width, "rotate_first", (1, 2))
    got = from_behind(mine_pass)
    near_shared, far_mine = share_first(after(slices, mine_pass))
    near = flat(swap_rows(near_shared))
    left = product(matrix, after(mine_keep, near_shared)[:width])
    far_mine = apply_got(after(far_mine, left), got)
    got_keep = from_behind(after(mine_keep, far_mine))
    far_mine = from_behind(far_mine)

    operands = (mine_keep, mine_pass, got, near)
    outs = (stacked, stacked, (half, half))
    next_pass, next_keep, mix, stat1 = rotation_call(second_body, flags[1], operands, outs, width, "rotate_second", (0, 1, 4, 5, 6))
    next_got = from_behind(next_pass)
    far = gather_rows(after(far_mine, next_pass))
    got_mix = from_behind(after(mix, next_pass))
    first_keep, first_got = after(mine_keep, next_pass), after(got, next_pass)
    right = product(behind, first_got[:width])
    received = from_behind(after(move(left, right, next_pass), next_got))
    both_kept = product_t(first_keep[:width], product(near, got_keep[:width]))

    operands = (next_keep, next_got, mine_keep, far, both_kept, got_keep, got_mix)
    outs = ((width, half), (width, half))
    pass_rot, keep_rot, stat2 = rotation_call(third_body, flags[2], operands, outs, width, "rotate_third", (0, 2))
    left = move(left, right, next_keep)
    moved = move(left, received, pass_rot)
    last = from_behind(moved)
    part = left_half(left, received, after(keep_rot, moved))
    stats, part = lax.optimization_barrier((jnp.concatenate([stat0, stat1, stat2], axis=1), part))
    sums = sum_over_pairs(stats).reshape(STEPS, TILE)
    rotated = join(part, last)
    return rotated, jnp.log(sums[:, 0] / sums[:, 1])


def solution(mesh):
    in_specs = (P("row", "col"), P())
    out_specs = (P("row", "col"), P())
    return jax.shard_map(
        on_device, mesh=mesh, in_specs=in_specs, out_specs=out_specs, check_vma=False
    )
```

```python
import functools

import jax
import jax.numpy as jnp
from jax import lax
from jax.experimental import pallas as pl
from jax.experimental.pallas import tpu as pltpu
from jax.sharding import PartitionSpec as P

SWEEPS = 2
STEPS = 3
SHARE_FLOPS = 2 * 10**10
EARLY_FLOPS = 2 * 10**9
TILE = 128
VMEM_LIMIT = 24 * 2**20

f32 = jnp.float32
bf16 = jnp.bfloat16
eps = 1e-06
in_smem = pl.BlockSpec(memory_space=pltpu.SMEM)


def split(x):
    high = x.astype(bf16)
    return high, (x - high.astype(f32)).astype(bf16)


def dot(first, second):
    return jnp.dot(first, second, preferred_element_type=f32)


def dot_t(first, second):
    return lax.dot_general(first, second, (((0,), (0,)), ((), ())), preferred_element_type=f32)


def triple(op, first, second):
    return op(first[0], second[0]) + (op(first[0], second[1]) + op(first[1], second[0]))


mul = functools.partial(triple, dot)
mul_t = functools.partial(triple, dot_t)


def columns(parts, start, size):
    return tuple(part[:, start : start + size] for part in parts)


in_any = pl.BlockSpec(memory_space=pl.ANY)
in_hbm = pl.BlockSpec(memory_space=pltpu.HBM)


def call(body, outs, operands, flops, name, scratch=(), flag=None, kept=()):
    single = not isinstance(outs, (list, tuple))
    results = [outs] if single else list(outs)
    count, total = len(operands), len(operands) + len(results)
    skip = 0 if flag is None else 1

    def run(*refs):
        flags, refs = refs[:skip], refs[skip:]
        far, near = refs[:total], refs[total : 2 * total]
        rest, sems = refs[2 * total : -1], refs[-1]
        copies = [pltpu.make_async_copy(far[i], near[i], sems.at[i]) for i in range(count)]
        for copy in copies:
            copy.start()
        for copy in copies:
            copy.wait()
        body(*flags, *near, *rest)
        copies = [pltpu.make_async_copy(near[i], far[i], sems.at[i]) for i in range(count, total)]
        for copy in copies:
            copy.start()
        for copy in copies:
            copy.wait()

    buffers = [pltpu.VMEM(x.shape, f32) for x in (*operands, *results)]
    made = pl.pallas_call(
        run,
        out_shape=results,
        in_specs=[in_smem] * skip + [in_hbm if i in kept else in_any for i in range(count)],
        out_specs=[in_hbm if i in kept else in_any for i in range(count, total)],
        scratch_shapes=[*buffers, *scratch, pltpu.SemaphoreType.DMA((total,))],
        compiler_params=pltpu.CompilerParams(vmem_limit_bytes=VMEM_LIMIT),
        cost_estimate=pl.CostEstimate(flops=flops, bytes_accessed=4 * 2**20, transcendentals=0),
        name=name,
    )(*(() if flag is None else (flag,)), *operands)
    return made[0] if single else made


def shape(*dims):
    return jax.ShapeDtypeStruct(dims, f32)


def tile_pairs(width):
    count = width // TILE
    return [(i, j) for i in range(count) for j in range(i, count)]


def gram_body(pair_ref, out_ref):
    parts = split(pair_ref[...])
    width = pair_ref.shape[1]
    half = width // 2
    blocks = {}
    for i, j in ((0, 0), (0, 1), (1, 1)):
        blocks[i, j] = mul_t(columns(parts, i * half, half), columns(parts, j * half, half))
    per = half // TILE
    for at, (i, j) in enumerate(tile_pairs(width)):
        block = blocks[i // per, j // per]
        r, c = (i % per) * TILE, (j % per) * TILE
        out_ref[at * TILE : (at + 1) * TILE, :] = block[r : r + TILE, c : c + TILE]


def local_gram(pair):
    rows, width = pair.shape
    count = len(tile_pairs(width))
    return call(gram_body, shape(count * TILE, TILE), [pair], 6 * rows * width * width, "local_gram")


def cross_body(mine_ref, ahead_ref, behind_ref, out_ref):
    behind = split(behind_ref[...])
    count, rows, _ = out_ref.shape
    part = rows // 2
    for at, ref in enumerate((mine_ref, ahead_ref)):
        made = mul_t(split(ref[...]), behind)
        for i in range(count):
            out_ref[i, at * part : (at + 1) * part, :] = made[i * part : (i + 1) * part, :]


def local_cross(mine, ahead, behind):
    rows, width = mine.shape
    count = lax.axis_size("row")
    out = shape(count, 2 * width // count, width)
    return call(cross_body, out, [mine, ahead, behind], 12 * rows * width * width, "local_cross")


def share_body(slices_ref, shared_ref, *others):
    count, part, _ = shared_ref.shape
    made = slices_ref[0]
    for i in range(1, count):
        made += slices_ref[i]
    for i in range(count):
        shared_ref[i] = made[:part]
    for ref in others:
        ref[...] = made[part:]


def share(slices, flops):
    return call(share_body, shape(*slices.shape), [slices], flops, "share")


def share_first(slices):
    count, rows, width = slices.shape
    outs = [shape(count, rows // 2, width), shape(rows // 2, width)]
    return call(share_body, outs, [slices], slices.size, "share_first")


def apply_body(mine_ref, got_ref, out_ref):
    out_ref[...] = mul(split(mine_ref[...]), split(got_ref[: mine_ref.shape[1], :]))


def apply_got(mine, got):
    out = shape(mine.shape[0], got.shape[1])
    return call(apply_body, out, [mine, got], EARLY_FLOPS, "apply_got")


def move_body(left_ref, right_ref, rot_ref, out_ref):
    half = rot_ref.shape[1]
    rot = split(rot_ref[: 2 * half, :])
    top, bottom = tuple(p[:half] for p in rot), tuple(p[half:] for p in rot)
    out_ref[...] = mul(split(left_ref[...]), top) + mul(split(right_ref[...]), bottom)


def move(left, right, rot):
    rows, half = left.shape
    return call(move_body, shape(rows, half), [left, right, rot], 12 * rows * half * half, "move")


def squared(parts):
    mixed = dot(parts[0], parts[1])
    return dot(parts[0], parts[0]) + (mixed + mixed.T)


def sweep(gram, row, col):
    eye = row == col
    one = eye.astype(f32)
    on_diag = jnp.where(eye, gram, 0.0)
    diag_sum = jnp.sum(on_diag, axis=0, keepdims=True) + jnp.sum(on_diag, axis=1, keepdims=True)
    ratio = gram / (diag_sum + eps)
    skew = jnp.where(col > row, ratio, jnp.where(row > col, -ratio, 0.0))
    norm = jnp.sum(jnp.sum(skew * skew, axis=0, keepdims=True), axis=1, keepdims=True)
    skew = skew * (1.0 / jnp.maximum(jnp.sqrt(norm), 1.0))
    skew_parts = split(skew)
    square = squared(skew_parts)
    square_parts = split(square)
    fourth = squared(square_parts)
    cube = mul(skew_parts, square_parts)
    low = one * (8.0 / 9.0) + (2.0 * fourth + 6.0 * square - 8.0 * skew - 4.0 * cube) * (2.0 / 9.0)
    z = (square + fourth) * (4.0 / 9.0)
    z_short = z.astype(bf16)
    y = z * (2.0 / 9.0) + dot(z_short, z_short)
    high = one * (820.0 / 729.0) + z * (82.0 / 81.0) + y * (10.0 / 9.0) + dot(z_short, y.astype(bf16))
    q_parts = split(mul(split(low), split(high)))
    return q_parts, mul(split(gram), q_parts)


def rotate(gram, stat_ref, last=False):
    width = gram.shape[0]
    half = width // 2
    row = lax.broadcasted_iota(jnp.int32, (width, width), 0)
    col = lax.broadcasted_iota(jnp.int32, (width, width), 1)
    first, half_turned = sweep(gram, row, col)
    gram = mul_t(first, split(half_turned))
    second, half_turned = sweep(gram, row, col)
    rotation = mul(first, second)
    turned = split(half_turned)
    left, right = columns(second, 0, half), columns(second, half, half)
    cross = mul_t(left, columns(turned, half, half))
    cross_sq = jnp.sum(jnp.sum(cross * cross, axis=0, keepdims=True), axis=1, keepdims=True)
    diag = jnp.sum((second[0].astype(f32) + second[1].astype(f32)) * half_turned, axis=0, keepdims=True)
    diag_sq = jnp.sum(diag * diag, axis=1, keepdims=True)
    lane = lax.broadcasted_iota(jnp.int32, stat_ref.shape, 1)
    stat_ref[...] = jnp.where(lane == 0, cross_sq, jnp.where(lane == 1, diag_sq, 0.0))
    if last:
        return rotation
    left_diag = mul_t(left, columns(turned, 0, half))
    right_diag = mul_t(right, columns(turned, half, half))
    return rotation, left_diag, cross, right_diag


def choose(flag, when_right, when_left, ref, at=0):
    ref[at : at + when_right.shape[0], :] = jnp.where(flag, when_right, when_left)


def give(flag, rotation, left_diag, right_diag, pass_ref, keep_ref):
    width = rotation.shape[0]
    half = width // 2
    choose(flag, rotation[:, half:], rotation[:, :half], pass_ref)
    choose(flag, right_diag, left_diag, pass_ref, width)
    choose(flag, rotation[:, :half], rotation[:, half:], keep_ref)
    choose(flag, left_diag, right_diag, keep_ref, width)


def set_gram(gram_ref, left_diag, cross, right_diag):
    half = cross.shape[0]
    gram_ref[:half, :half] = left_diag
    gram_ref[:half, half:] = cross
    gram_ref[half:, :half] = cross.T
    gram_ref[half:, half:] = right_diag


def first_body(flag_ref, tiles_ref, pass_ref, keep_ref, stat_ref, gram_ref):
    for at, (i, j) in enumerate(tile_pairs(gram_ref.shape[0])):
        tile = tiles_ref[at * TILE : (at + 1) * TILE, :]
        gram_ref[i * TILE : (i + 1) * TILE, j * TILE : (j + 1) * TILE] = tile
        if i != j:
            gram_ref[j * TILE : (j + 1) * TILE, i * TILE : (i + 1) * TILE] = tile.T
    flag = flag_ref[0] == 1
    rotation, left_diag, cross, right_diag = rotate(gram_ref[...], stat_ref)
    give(flag, rotation, left_diag, right_diag, pass_ref, keep_ref)
    choose(flag, cross, cross.T, keep_ref, pass_ref.shape[0])


def second_body(flag_ref, mine_keep_ref, mine_pass_ref, got_ref, near_ref, pass_ref, keep_ref, mix_ref, stat_ref, gram_ref):
    width = gram_ref.shape[0]
    half = width // 2
    inner = split(mul(split(near_ref[...]), split(got_ref[:width, :])))
    cross = mul_t(split(mine_keep_ref[:width, :]), inner)
    mix_ref[...] = mul_t(split(mine_pass_ref[:width, :]), inner)
    set_gram(gram_ref, mine_keep_ref[width : width + half, :], cross, got_ref[width:, :])
    flag = flag_ref[0] == 1
    rotation, left_diag, _, right_diag = rotate(gram_ref[...], stat_ref)
    give(flag, rotation, left_diag, right_diag, pass_ref, keep_ref)


def third_body(
    flag_ref, keep1_ref, got1_ref, keep0_ref, far_ref, both_kept_ref, off_ref, mix_ref,
    pass_rot_ref, keep_rot_ref, stat_ref, gram_ref,
):
    width = gram_ref.shape[0]
    half = width // 2
    top, bottom = split(got1_ref[:half, :]), split(got1_ref[half:width, :])
    through = mul(split(far_ref[...]), bottom)
    upper = mul(split(both_kept_ref[...]), top) + mul_t(split(keep0_ref[:width, :]), split(through))
    lower = mul_t(split(off_ref[-half:, :]), top) + mul(split(mix_ref[...]), bottom)
    cross = mul_t(split(keep1_ref[:half, :]), split(upper)) + mul_t(split(keep1_ref[half:width, :]), split(lower))
    set_gram(gram_ref, keep1_ref[width:, :], cross, got1_ref[width:, :])
    flag = flag_ref[0] == 1
    rotation = rotate(gram_ref[...], stat_ref, last=True)
    choose(flag, rotation[:, half:], rotation[:, :half], pass_rot_ref)
    choose(flag, rotation[:, :half], rotation[:, half:], keep_rot_ref)


def rotation_call(body, flag, operands, outs, width, name, kept):
    outs = [shape(*dims) for dims in outs] + [shape(1, TILE)]
    scratch = [pltpu.VMEM((width, width), f32)]
    return call(body, outs, operands, 88 * width**3, name, scratch, flag, kept)


def product(first, second):
    return jnp.dot(first, second, precision=lax.Precision.HIGH, preferred_element_type=f32)


def product_t(first, second):
    dims = (((0,), (0,)), ((), ()))
    return lax.dot_general(first, second, dims, precision=lax.Precision.HIGH, preferred_element_type=f32)


def left_body(left_ref, right_ref, rot_ref, out_ref, left, right, rot, made, sems):
    copies = [
        pltpu.make_async_copy(far, near, sems.at[i])
        for i, (far, near) in enumerate(((left_ref, left), (right_ref, right), (rot_ref, rot)))
    ]
    for copy in copies:
        copy.start()
    for copy in copies:
        copy.wait()
    move_body(left, right, rot, made)
    copy = pltpu.make_async_copy(made, out_ref.at[:, : made.shape[1]], sems.at[3])
    copy.start()
    copy.wait()


def left_half(left, right, rot):
    rows, half = left.shape
    buffers = [pltpu.VMEM(x.shape, f32) for x in (left, right, rot, left)]
    return pl.pallas_call(
        left_body,
        out_shape=shape(rows, 2 * half),
        in_specs=[in_any] * 3,
        out_specs=in_any,
        scratch_shapes=[*buffers, pltpu.SemaphoreType.DMA((4,))],
        compiler_params=pltpu.CompilerParams(vmem_limit_bytes=VMEM_LIMIT),
        cost_estimate=pl.CostEstimate(flops=SHARE_FLOPS, bytes_accessed=4 * 2**20, transcendentals=0),
        name="left_half",
    )(left, right, rot)


def join_body(part_ref, right_ref, out_ref, right, sems):
    copy = pltpu.make_async_copy(right_ref, right, sems.at[0])
    copy.start()
    copy.wait()
    copy = pltpu.make_async_copy(right, out_ref.at[:, right.shape[1] :], sems.at[1])
    copy.start()
    copy.wait()


def join(part, right):
    return pl.pallas_call(
        join_body,
        out_shape=shape(*part.shape),
        in_specs=[in_any] * 2,
        out_specs=in_any,
        scratch_shapes=[pltpu.VMEM(right.shape, f32), pltpu.SemaphoreType.DMA((2,))],
        input_output_aliases={0: 0},
        name="join",
    )(part, right)


def from_behind(x, by=1):
    count = lax.axis_size("col")
    return lax.ppermute(x, "col", [(i, (i + by) % count) for i in range(count)])


def swap_rows(slices):
    return lax.all_to_all(slices, "row", 0, 0)


def flat(slices):
    return slices.reshape(slices.shape[0] * slices.shape[1], slices.shape[2])


def gather_rows(mine):
    count = lax.axis_size("row")
    return flat(swap_rows(jnp.broadcast_to(mine[None], (count, *mine.shape))))


def sum_over_pairs(x):
    count = lax.axis_size("col")
    shared = jnp.broadcast_to(x, (count, x.shape[1]))
    return jnp.sum(lax.all_to_all(shared, "col", 0, 0, tiled=True), axis=0)


def after(x, *others):
    return lax.optimization_barrier((x, *others))[0]


def on_device(matrix, plan):
    rows, width = matrix.shape
    half = width // 2
    stacked = (width + half, half)
    position = lax.axis_index("col")
    flags = lax.dynamic_slice_in_dim(plan, position, 1, axis=1)

    behind = from_behind(matrix)
    ahead = from_behind(matrix, -1)
    tiles = local_gram(matrix)
    count = lax.axis_size("row")
    slices = swap_rows(tiles.reshape(count, tiles.shape[0] // count, TILE))
    gram = flat(swap_rows(share(slices, SHARE_FLOPS)))
    slices = swap_rows(local_cross(matrix, ahead, behind))

    outs = (stacked, (2 * width, half))
    mine_pass, mine_keep, stat0 = rotation_call(first_body, flags[0], (gram,), outs, width, "rotate_first", (1, 2))
    got = from_behind(mine_pass)
    near_shared, far_mine = share_first(after(slices, mine_pass))
    near = flat(swap_rows(near_shared))
    left = product(matrix, after(mine_keep, near_shared)[:width])
    far_mine = apply_got(after(far_mine, left), got)
    got_keep = from_behind(after(mine_keep, far_mine))
    far_mine = from_behind(far_mine)

    operands = (mine_keep, mine_pass, got, near)
    outs = (stacked, stacked, (half, half))
    next_pass, next_keep, mix, stat1 = rotation_call(second_body, flags[1], operands, outs, width, "rotate_second", (0, 1, 4, 5, 6))
    next_got = from_behind(next_pass)
    far = gather_rows(after(far_mine, next_pass))
    got_mix = from_behind(after(mix, next_pass))
    first_keep, first_got = after(mine_keep, next_pass), after(got, next_pass)
    right = product(behind, first_got[:width])
    received = from_behind(after(move(left, right, next_pass), next_got))
    both_kept = product_t(first_keep[:width], product(near, got_keep[:width]))

    operands = (next_keep, next_got, mine_keep, far, both_kept, got_keep, got_mix)
    outs = ((width, half), (width, half))
    pass_rot, keep_rot, stat2 = rotation_call(third_body, flags[2], operands, outs, width, "rotate_third", (0, 2))
    left = move(left, right, next_keep)
    moved = move(left, received, pass_rot)
    last = from_behind(moved)
    part = left_half(left, received, after(keep_rot, moved))
    stats = after(jnp.concatenate([stat0, stat1, stat2], axis=1), moved)
    sums = sum_over_pairs(stats).reshape(STEPS, TILE)
    rotated = join(part, last)
    return rotated, jnp.log(sums[:, 0] / sums[:, 1])


def solution(mesh):
    in_specs = (P("row", "col"), P())
    out_specs = (P("row", "col"), P())
    return jax.shard_map(
        on_device, mesh=mesh, in_specs=in_specs, out_specs=out_specs, check_vma=False
    )
```

```python
import functools

import jax
import jax.numpy as jnp
from jax import lax
from jax.experimental import pallas as pl
from jax.experimental.pallas import tpu as pltpu
from jax.sharding import PartitionSpec as P

SWEEPS = 2
STEPS = 3
SHARE_FLOPS = 2 * 10**10
EARLY_FLOPS = 2 * 10**9
TILE = 128
VMEM_LIMIT = 24 * 2**20
VMEM_WHOLE = 58 * 2**20

f32 = jnp.float32
bf16 = jnp.bfloat16
eps = 1e-06
in_smem = pl.BlockSpec(memory_space=pltpu.SMEM)


def split(x):
    high = x.astype(bf16)
    return high, (x - high.astype(f32)).astype(bf16)


def dot(first, second):
    return jnp.dot(first, second, preferred_element_type=f32)


def dot_t(first, second):
    return lax.dot_general(first, second, (((0,), (0,)), ((), ())), preferred_element_type=f32)


def triple(op, first, second):
    return op(first[0], second[0]) + (op(first[0], second[1]) + op(first[1], second[0]))


mul = functools.partial(triple, dot)
mul_t = functools.partial(triple, dot_t)


def columns(parts, start, size):
    return tuple(part[:, start : start + size] for part in parts)


in_any = pl.BlockSpec(memory_space=pl.ANY)
in_hbm = pl.BlockSpec(memory_space=pltpu.HBM)


def call(body, outs, operands, flops, name, scratch=(), flag=None, kept=()):
    single = not isinstance(outs, (list, tuple))
    results = [outs] if single else list(outs)
    count, total = len(operands), len(operands) + len(results)
    skip = 0 if flag is None else 1

    def run(*refs):
        flags, refs = refs[:skip], refs[skip:]
        far, near = refs[:total], refs[total : 2 * total]
        rest, sems = refs[2 * total : -1], refs[-1]
        copies = [pltpu.make_async_copy(far[i], near[i], sems.at[i]) for i in range(count)]
        for copy in copies:
            copy.start()
        for copy in copies:
            copy.wait()
        body(*flags, *near, *rest)
        copies = [pltpu.make_async_copy(near[i], far[i], sems.at[i]) for i in range(count, total)]
        for copy in copies:
            copy.start()
        for copy in copies:
            copy.wait()

    buffers = [pltpu.VMEM(x.shape, f32) for x in (*operands, *results)]
    made = pl.pallas_call(
        run,
        out_shape=results,
        in_specs=[in_smem] * skip + [in_hbm if i in kept else in_any for i in range(count)],
        out_specs=[in_hbm if i in kept else in_any for i in range(count, total)],
        scratch_shapes=[*buffers, *scratch, pltpu.SemaphoreType.DMA((total,))],
        compiler_params=pltpu.CompilerParams(vmem_limit_bytes=VMEM_LIMIT),
        cost_estimate=pl.CostEstimate(flops=flops, bytes_accessed=4 * 2**20, transcendentals=0),
        name=name,
    )(*(() if flag is None else (flag,)), *operands)
    return made[0] if single else made


def shape(*dims):
    return jax.ShapeDtypeStruct(dims, f32)


def tile_pairs(width):
    count = width // TILE
    return [(i, j) for i in range(count) for j in range(i, count)]


def gram_body(pair_ref, out_ref):
    parts = split(pair_ref[...])
    width = pair_ref.shape[1]
    half = width // 2
    blocks = {}
    for i, j in ((0, 0), (0, 1), (1, 1)):
        blocks[i, j] = mul_t(columns(parts, i * half, half), columns(parts, j * half, half))
    per = half // TILE
    for at, (i, j) in enumerate(tile_pairs(width)):
        block = blocks[i // per, j // per]
        r, c = (i % per) * TILE, (j % per) * TILE
        out_ref[at * TILE : (at + 1) * TILE, :] = block[r : r + TILE, c : c + TILE]


def local_gram(pair):
    rows, width = pair.shape
    count = len(tile_pairs(width))
    return call(gram_body, shape(count * TILE, TILE), [pair], 6 * rows * width * width, "local_gram")


def cross_body(mine_ref, ahead_ref, behind_ref, out_ref, mine, ahead, behind, near, far, sems):
    fetches = [
        pltpu.make_async_copy(source, target, sems.at[i])
        for i, (source, target) in enumerate(((behind_ref, behind), (mine_ref, mine), (ahead_ref, ahead)))
    ]
    for copy in fetches:
        copy.start()
    fetches[0].wait()
    right = split(behind[...])
    count, part, _ = near.shape
    stores = []
    for at, (columns_ref, made_ref) in enumerate(((mine, near), (ahead, far))):
        fetches[at + 1].wait()
        made = mul_t(split(columns_ref[...]), right)
        for i in range(count):
            made_ref[i] = made[i * part : (i + 1) * part, :]
        stores.append(pltpu.make_async_copy(made_ref, out_ref.at[:, at * part : (at + 1) * part, :], sems.at[3 + at]))
        stores[at].start()
    for copy in stores:
        copy.wait()


def local_cross(mine, ahead, behind):
    rows, width = mine.shape
    count = lax.axis_size("row")
    part = width // count
    buffers = [pltpu.VMEM((rows, width), f32)] * 3 + [pltpu.VMEM((count, part, width), f32)] * 2
    return pl.pallas_call(
        cross_body,
        out_shape=shape(count, 2 * part, width),
        in_specs=[in_any] * 3,
        out_specs=in_any,
        scratch_shapes=[*buffers, pltpu.SemaphoreType.DMA((5,))],
        compiler_params=pltpu.CompilerParams(vmem_limit_bytes=VMEM_WHOLE),
        cost_estimate=pl.CostEstimate(flops=12 * rows * width * width, bytes_accessed=4 * 2**20, transcendentals=0),
        name="local_cross",
    )(mine, ahead, behind)


def share_body(slices_ref, shared_ref, *others):
    count, part, _ = shared_ref.shape
    made = slices_ref[0]
    for i in range(1, count):
        made += slices_ref[i]
    for i in range(count):
        shared_ref[i] = made[:part]
    for ref in others:
        ref[...] = made[part:]


def share(slices, flops):
    return call(share_body, shape(*slices.shape), [slices], flops, "share")


def share_first(slices):
    count, rows, width = slices.shape
    outs = [shape(count, rows // 2, width), shape(rows // 2, width)]
    return call(share_body, outs, [slices], slices.size, "share_first")


def apply_body(mine_ref, got_ref, out_ref):
    out_ref[...] = mul(split(mine_ref[...]), split(got_ref[: mine_ref.shape[1], :]))


def apply_got(mine, got):
    out = shape(mine.shape[0], got.shape[1])
    return call(apply_body, out, [mine, got], EARLY_FLOPS, "apply_got")


def move_body(left_ref, right_ref, rot_ref, out_ref):
    half = rot_ref.shape[1]
    rot = split(rot_ref[: 2 * half, :])
    top, bottom = tuple(p[:half] for p in rot), tuple(p[half:] for p in rot)
    out_ref[...] = mul(split(left_ref[...]), top) + mul(split(right_ref[...]), bottom)


def move(left, right, rot):
    rows, half = left.shape
    return call(move_body, shape(rows, half), [left, right, rot], 12 * rows * half * half, "move")


def squared(parts):
    mixed = dot(parts[0], parts[1])
    return dot(parts[0], parts[0]) + (mixed + mixed.T)


def sweep(gram, row, col):
    eye = row == col
    one = eye.astype(f32)
    on_diag = jnp.where(eye, gram, 0.0)
    diag_sum = jnp.sum(on_diag, axis=0, keepdims=True) + jnp.sum(on_diag, axis=1, keepdims=True)
    ratio = gram / (diag_sum + eps)
    skew = jnp.where(col > row, ratio, jnp.where(row > col, -ratio, 0.0))
    norm = jnp.sum(jnp.sum(skew * skew, axis=0, keepdims=True), axis=1, keepdims=True)
    skew = skew * (1.0 / jnp.maximum(jnp.sqrt(norm), 1.0))
    skew_parts = split(skew)
    square = squared(skew_parts)
    square_parts = split(square)
    fourth = squared(square_parts)
    cube = mul(skew_parts, square_parts)
    low = one * (8.0 / 9.0) + (2.0 * fourth + 6.0 * square - 8.0 * skew - 4.0 * cube) * (2.0 / 9.0)
    z = (square + fourth) * (4.0 / 9.0)
    z_short = z.astype(bf16)
    y = z * (2.0 / 9.0) + dot(z_short, z_short)
    high = one * (820.0 / 729.0) + z * (82.0 / 81.0) + y * (10.0 / 9.0) + dot(z_short, y.astype(bf16))
    q_parts = split(mul(split(low), split(high)))
    return q_parts, mul(split(gram), q_parts)


def rotate(gram, stat_ref, last=False):
    width = gram.shape[0]
    half = width // 2
    row = lax.broadcasted_iota(jnp.int32, (width, width), 0)
    col = lax.broadcasted_iota(jnp.int32, (width, width), 1)
    first, half_turned = sweep(gram, row, col)
    gram = mul_t(first, split(half_turned))
    second, half_turned = sweep(gram, row, col)
    rotation = mul(first, second)
    turned = split(half_turned)
    left, right = columns(second, 0, half), columns(second, half, half)
    cross = mul_t(left, columns(turned, half, half))
    cross_sq = jnp.sum(jnp.sum(cross * cross, axis=0, keepdims=True), axis=1, keepdims=True)
    diag = jnp.sum((second[0].astype(f32) + second[1].astype(f32)) * half_turned, axis=0, keepdims=True)
    diag_sq = jnp.sum(diag * diag, axis=1, keepdims=True)
    lane = lax.broadcasted_iota(jnp.int32, stat_ref.shape, 1)
    stat_ref[...] = jnp.where(lane == 0, cross_sq, jnp.where(lane == 1, diag_sq, 0.0))
    if last:
        return rotation
    left_diag = mul_t(left, columns(turned, 0, half))
    right_diag = mul_t(right, columns(turned, half, half))
    return rotation, left_diag, cross, right_diag


def choose(flag, when_right, when_left, ref, at=0):
    ref[at : at + when_right.shape[0], :] = jnp.where(flag, when_right, when_left)


def give(flag, rotation, left_diag, right_diag, pass_ref, keep_ref):
    width = rotation.shape[0]
    half = width // 2
    choose(flag, rotation[:, half:], rotation[:, :half], pass_ref)
    choose(flag, right_diag, left_diag, pass_ref, width)
    choose(flag, rotation[:, :half], rotation[:, half:], keep_ref)
    choose(flag, left_diag, right_diag, keep_ref, width)


def set_gram(gram_ref, left_diag, cross, right_diag):
    half = cross.shape[0]
    gram_ref[:half, :half] = left_diag
    gram_ref[:half, half:] = cross
    gram_ref[half:, :half] = cross.T
    gram_ref[half:, half:] = right_diag


def first_body(flag_ref, tiles_ref, pass_ref, keep_ref, stat_ref, gram_ref):
    for at, (i, j) in enumerate(tile_pairs(gram_ref.shape[0])):
        tile = tiles_ref[at * TILE : (at + 1) * TILE, :]
        gram_ref[i * TILE : (i + 1) * TILE, j * TILE : (j + 1) * TILE] = tile
        if i != j:
            gram_ref[j * TILE : (j + 1) * TILE, i * TILE : (i + 1) * TILE] = tile.T
    flag = flag_ref[0] == 1
    rotation, left_diag, cross, right_diag = rotate(gram_ref[...], stat_ref)
    give(flag, rotation, left_diag, right_diag, pass_ref, keep_ref)
    choose(flag, cross, cross.T, keep_ref, pass_ref.shape[0])


def second_body(flag_ref, mine_keep_ref, mine_pass_ref, got_ref, near_ref, pass_ref, keep_ref, mix_ref, stat_ref, gram_ref):
    width = gram_ref.shape[0]
    half = width // 2
    inner = split(mul(split(near_ref[...]), split(got_ref[:width, :])))
    cross = mul_t(split(mine_keep_ref[:width, :]), inner)
    mix_ref[...] = mul_t(split(mine_pass_ref[:width, :]), inner)
    set_gram(gram_ref, mine_keep_ref[width : width + half, :], cross, got_ref[width:, :])
    flag = flag_ref[0] == 1
    rotation, left_diag, _, right_diag = rotate(gram_ref[...], stat_ref)
    give(flag, rotation, left_diag, right_diag, pass_ref, keep_ref)


def third_body(
    flag_ref, keep1_ref, got1_ref, keep0_ref, far_ref, both_kept_ref, off_ref, mix_ref,
    pass_rot_ref, keep_rot_ref, stat_ref, gram_ref,
):
    width = gram_ref.shape[0]
    half = width // 2
    top, bottom = split(got1_ref[:half, :]), split(got1_ref[half:width, :])
    through = mul(split(far_ref[...]), bottom)
    upper = mul(split(both_kept_ref[...]), top) + mul_t(split(keep0_ref[:width, :]), split(through))
    lower = mul_t(split(off_ref[-half:, :]), top) + mul(split(mix_ref[...]), bottom)
    cross = mul_t(split(keep1_ref[:half, :]), split(upper)) + mul_t(split(keep1_ref[half:width, :]), split(lower))
    set_gram(gram_ref, keep1_ref[width:, :], cross, got1_ref[width:, :])
    flag = flag_ref[0] == 1
    rotation = rotate(gram_ref[...], stat_ref, last=True)
    choose(flag, rotation[:, half:], rotation[:, :half], pass_rot_ref)
    choose(flag, rotation[:, :half], rotation[:, half:], keep_rot_ref)


def rotation_call(body, flag, operands, outs, width, name, kept):
    outs = [shape(*dims) for dims in outs] + [shape(1, TILE)]
    scratch = [pltpu.VMEM((width, width), f32)]
    return call(body, outs, operands, 88 * width**3, name, scratch, flag, kept)


def product(first, second):
    return jnp.dot(first, second, precision=lax.Precision.HIGH, preferred_element_type=f32)


def product_t(first, second):
    dims = (((0,), (0,)), ((), ()))
    return lax.dot_general(first, second, dims, precision=lax.Precision.HIGH, preferred_element_type=f32)


def left_body(left_ref, right_ref, rot_ref, out_ref, left, right, rot, made, sems):
    copies = [
        pltpu.make_async_copy(far, near, sems.at[i])
        for i, (far, near) in enumerate(((left_ref, left), (right_ref, right), (rot_ref, rot)))
    ]
    for copy in copies:
        copy.start()
    for copy in copies:
        copy.wait()
    move_body(left, right, rot, made)
    copy = pltpu.make_async_copy(made, out_ref.at[:, : made.shape[1]], sems.at[3])
    copy.start()
    copy.wait()


def left_half(left, right, rot):
    rows, half = left.shape
    buffers = [pltpu.VMEM(x.shape, f32) for x in (left, right, rot, left)]
    return pl.pallas_call(
        left_body,
        out_shape=shape(rows, 2 * half),
        in_specs=[in_any] * 3,
        out_specs=in_any,
        scratch_shapes=[*buffers, pltpu.SemaphoreType.DMA((4,))],
        compiler_params=pltpu.CompilerParams(vmem_limit_bytes=VMEM_LIMIT),
        cost_estimate=pl.CostEstimate(flops=SHARE_FLOPS, bytes_accessed=4 * 2**20, transcendentals=0),
        name="left_half",
    )(left, right, rot)


def join_body(part_ref, right_ref, out_ref, right, sems):
    copy = pltpu.make_async_copy(right_ref, right, sems.at[0])
    copy.start()
    copy.wait()
    copy = pltpu.make_async_copy(right, out_ref.at[:, right.shape[1] :], sems.at[1])
    copy.start()
    copy.wait()


def join(part, right):
    return pl.pallas_call(
        join_body,
        out_shape=shape(*part.shape),
        in_specs=[in_any] * 2,
        out_specs=in_any,
        scratch_shapes=[pltpu.VMEM(right.shape, f32), pltpu.SemaphoreType.DMA((2,))],
        input_output_aliases={0: 0},
        name="join",
    )(part, right)


def from_behind(x, by=1):
    count = lax.axis_size("col")
    return lax.ppermute(x, "col", [(i, (i + by) % count) for i in range(count)])


def swap_rows(slices):
    return lax.all_to_all(slices, "row", 0, 0)


def flat(slices):
    return slices.reshape(slices.shape[0] * slices.shape[1], slices.shape[2])


def gather_rows(mine):
    count = lax.axis_size("row")
    return flat(swap_rows(jnp.broadcast_to(mine[None], (count, *mine.shape))))


def sum_over_pairs(x):
    count = lax.axis_size("col")
    shared = jnp.broadcast_to(x, (count, x.shape[1]))
    return jnp.sum(lax.all_to_all(shared, "col", 0, 0, tiled=True), axis=0)


def after(x, *others):
    return lax.optimization_barrier((x, *others))[0]


def on_device(matrix, plan):
    rows, width = matrix.shape
    half = width // 2
    stacked = (width + half, half)
    position = lax.axis_index("col")
    flags = lax.dynamic_slice_in_dim(plan, position, 1, axis=1)

    behind = from_behind(matrix)
    ahead = from_behind(matrix, -1)
    tiles = local_gram(matrix)
    count = lax.axis_size("row")
    slices = swap_rows(tiles.reshape(count, tiles.shape[0] // count, TILE))
    gram = flat(swap_rows(share(slices, SHARE_FLOPS)))
    slices = swap_rows(local_cross(matrix, ahead, behind))

    outs = (stacked, (2 * width, half))
    mine_pass, mine_keep, stat0 = rotation_call(first_body, flags[0], (gram,), outs, width, "rotate_first", (1, 2))
    got = from_behind(mine_pass)
    near_shared, far_mine = share_first(after(slices, mine_pass))
    near = flat(swap_rows(near_shared))
    left = product(matrix, after(mine_keep, near_shared)[:width])
    far_mine = apply_got(after(far_mine, left), got)
    got_keep = from_behind(after(mine_keep, far_mine))
    far_mine = from_behind(far_mine)

    operands = (mine_keep, mine_pass, got, near)
    outs = (stacked, stacked, (half, half))
    next_pass, next_keep, mix, stat1 = rotation_call(second_body, flags[1], operands, outs, width, "rotate_second", (0, 1, 4, 5, 6))
    next_got = from_behind(next_pass)
    far = gather_rows(after(far_mine, next_pass))
    got_mix = from_behind(after(mix, next_pass))
    first_keep, first_got = after(mine_keep, next_pass), after(got, next_pass)
    right = product(behind, first_got[:width])
    received = from_behind(after(move(left, right, next_pass), next_got))
    both_kept = product_t(first_keep[:width], product(near, got_keep[:width]))

    operands = (next_keep, next_got, mine_keep, far, both_kept, got_keep, got_mix)
    outs = ((width, half), (width, half))
    pass_rot, keep_rot, stat2 = rotation_call(third_body, flags[2], operands, outs, width, "rotate_third", (0, 2))
    left = move(left, right, next_keep)
    moved = move(left, received, pass_rot)
    last = from_behind(moved)
    part = left_half(left, received, after(keep_rot, moved))
    stats = after(jnp.concatenate([stat0, stat1, stat2], axis=1), moved)
    sums = sum_over_pairs(stats).reshape(STEPS, TILE)
    rotated = join(part, last)
    return rotated, jnp.log(sums[:, 0] / sums[:, 1])


def solution(mesh):
    in_specs = (P("row", "col"), P())
    out_specs = (P("row", "col"), P())
    return jax.shard_map(
        on_device, mesh=mesh, in_specs=in_specs, out_specs=out_specs, check_vma=False
    )
```
